512 devices in a mesh: var: 32 (over x, z_lo), smp: 16 (over z_hi, y, core).
Axes of the slice: x: 4, y: 4, z: 16 (z_hi: 2, z_lo: 8; z = z_hi * 8 + z_lo), core: 2. Of those that a mesh axis runs over, the one named last changes fastest.
Arguments:
- dosages: bfloat16 [8192, 16384], P('var', 'smp'), may hold values from 0 to 2
- band_counts: int32 [64], P('var'), may hold values from 512 to 2048, as said below
Outputs:
- upper: float32 [8192, 2048], P('var', 'smp')
- lower: float32 [8192, 2048], P('var', 'smp')
The draws below stay inside these ranges and needn't reach their ends.
Inputs may be any that keep to these rules, and one draw needn't show every extreme that they name: `band_counts`: every value lies in 512 to 2048; both ends are taken by some block.
All inputs are finite; a program needn't handle non-finite values.
Results may differ from the reference program's by a relative error of at most 0.0005.
The reference program's roundings to bfloat16 on the way (of `scaled`) count: a program that leaves them out, or rounds other values in their place, can miss the bound.
Values may be sent and summed in bfloat16 or wider, within the bound.
A program may use at most 64 MiB of HBM per device.

```python
import jax
import jax.numpy as jnp
from jax import lax

M_DEV = 256
W = 2048
BLK = 128
M = 8192
N = 16384


def draw_dosages(key, part):
    key = jax.random.fold_in(key, 11)
    keys = jax.random.split(key, 4)
    step_fine = 64
    coarse = jax.random.normal(keys[0], (M // W + 2, N), jnp.float32)
    fine = jax.random.normal(keys[1], (M // step_fine + 2, N), jnp.float32)
    noise = jax.random.normal(keys[2], (M, N), jnp.float32)
    spots = jnp.arange(M, dtype=jnp.int32)
    low_c = spots // W
    frac_c = ((spots % W).astype(jnp.float32) / W)[:, None]
    low_f = spots // step_fine
    frac_f = ((spots % step_fine).astype(jnp.float32) / step_fine)[:, None]
    coarse_part = (1.0 - frac_c) * coarse[low_c] + frac_c * coarse[low_c + 1]
    fine_part = (1.0 - frac_f) * fine[low_f] + frac_f * fine[low_f + 1]
    freq = jax.random.uniform(keys[3], (M, 1), jnp.float32, 0.15, 0.85)
    deviation = 0.45 * coarse_part + 0.35 * fine_part + 0.5 * noise
    return jnp.clip(2.0 * freq + 0.4 * deviation, 0.0, 2.0).astype(jnp.bfloat16)


def draw_band_counts(key, part):
    key = jax.random.fold_in(key, 23)
    keys = jax.random.split(key, 3)
    blocks = M // BLK
    counts = jax.random.randint(keys[0], (blocks,), W // 4, W + 1)
    first = jax.random.randint(keys[1], (), 0, blocks)
    second = (first + 1 + jax.random.randint(keys[2], (), 0, blocks - 1)) % blocks
    places = jnp.arange(blocks, dtype=jnp.int32)
    counts = jnp.where(places == first, W, counts)
    counts = jnp.where(places == second, W // 4, counts)
    return counts.astype(jnp.int32)


def setup_inputs(seed: int = 0) -> dict:
    streams_of = jax.random.split(jax.random.key(seed), 3)
    dosages = draw_dosages(jax.random.fold_in(streams_of[2], 71), 0)
    band_counts = draw_band_counts(jax.random.fold_in(streams_of[2], 71), 0)
    return {"dosages": dosages, "band_counts": band_counts}


def skew_forward(products, span):
    count, width = products.shape
    flat = jnp.concatenate([products.reshape(-1), jnp.zeros((count + 1,), jnp.float32)])
    return flat[1:1 + count * (width + 1)].reshape(count, width + 1)[:, :span]

def reference(dosages, band_counts):
    values = dosages.astype(jnp.float32)
    total = values.shape[0]
    samples = values.shape[1]
    means = lax.optimization_barrier(jnp.sum(values, axis=1, keepdims=True)) / samples
    centred = values - means
    spread = lax.optimization_barrier(jnp.sum(centred * centred, axis=1, keepdims=True)) / samples
    scaled = (centred * lax.rsqrt(spread + 1e-05)).astype(jnp.bfloat16)
    padded = jnp.concatenate([scaled, jnp.zeros((W + M_DEV, samples), jnp.bfloat16)], 0)

    def one_block(index):
        begin = (index * M_DEV).astype(jnp.int32)
        own = lax.dynamic_slice_in_dim(padded, begin, M_DEV, 0)
        later = lax.dynamic_slice_in_dim(padded, begin, M_DEV + W, 0)
        products = lax.dot_general(own, later, (((1,), (1,)), ((), ())), preferred_element_type=jnp.float32) / samples
        return skew_forward(products, W)
    banded = lax.map(one_block, jnp.arange(total // M_DEV, dtype=jnp.int32)).reshape(total, W)
    row_ids = lax.broadcasted_iota(jnp.int32, (total, W), 0)
    offsets = lax.broadcasted_iota(jnp.int32, (total, W), 1)
    row_counts = jnp.repeat(band_counts, BLK)[:, None]
    keep = (offsets < row_counts) & (row_ids + 1 + offsets < total)
    upper = jnp.where(keep, banded, jnp.float32(0.0))
    shifted = jnp.concatenate([jnp.zeros((W, W), jnp.float32), upper], 0)
    index = row_ids + W - 1 - offsets
    lower = jnp.take_along_axis(shifted, index, axis=0)
    return (upper, lower)
```

```python
import functools

import jax
import jax.numpy as jnp
from jax import lax
from jax.experimental import pallas as pl
from jax.experimental.pallas import tpu as pltpu
from jax.sharding import PartitionSpec as P

W = 2048
BLK = 128
LINE = 8
YS = 4
CHUNKS = 4
FOLD, GIVE, TAKE = 1, 3, 6
MESH = pl.DeviceIdType.MESH


def skew(tile):
    n = tile.shape[1]
    sub = lax.broadcasted_iota(jnp.int32, (8, n), 0)
    parts = []
    for at in range(0, tile.shape[0], 8):
        part = pltpu.roll(tile[at : at + 8], (2 * n - at - 1) % n, 1)
        for step in (1, 2, 4):
            part = jnp.where((sub & step) != 0, pltpu.roll(part, n - step, 1), part)
        parts.append(part)
    return jnp.concatenate(parts, 0)


def unshear(window, rows):
    height, n = window.shape
    lag = n - 1 - lax.broadcasted_iota(jnp.int32, (height, n), 1)
    step = 1
    while step < n:
        moved = pltpu.roll(window, height - step, 0)
        window = jnp.where((lag & step) != 0, moved, window)
        step *= 2
    return window[:rows]


DOWN, UP, BACK, FORE = range(4)
ONE_ON, TWO_ON, HIGH_ON, BEHIND = 8, 9, 10, 11
SLOTS = 12
REACH = 9
PHASES = 4
TASKS = 16


def kernel(
    total_samples, total_rows,
    dosages, counts, upper, lower,
    raw, ready, mine, twin, shares, part, other, across, arrived, window, stat_out, stat_in, facts,
    stat_ss, stat_rs, raw_ss, raw_rs, fact_ss, fact_rs,
    twin_ss, twin_rs, share_ss, share_rs, give_ss, give_rs, end_ss, end_rs,
):
    rows, cols = dosages.shape
    v = lax.axis_index("var")
    s = lax.axis_index("smp")
    x, z = v // LINE, v % LINE
    hi, y, core = s // (2 * YS), (s // 2) % YS, s % 2
    lines = total_rows // rows // LINE
    blocks = lines * LINE
    mid = LINE // 2
    smps = 4 * YS
    group = hi * YS + y
    chunk = rows // CHUNKS
    width = upper.shape[1]
    f32 = jnp.float32
    low = z < mid
    first_line, last_line = x == 0, x == lines - 1
    pick = jnp.where

    def there(d):
        return (d != 0) & (v + d >= 0) & (v + d < blocks)

    barrier = pltpu.get_barrier_semaphore()
    for step in range(smps // 2, smps + smps // 2):
        if step != smps:
            peer = lax.rem(s + step, smps)
            pl.semaphore_signal(barrier, inc=1, device_id=(v, peer), device_id_type=MESH)

    def greet(n, carry):
        d = n - REACH

        @pl.when(there(d))
        def _():
            pl.semaphore_signal(barrier, inc=1, device_id=(v + d, s), device_id_type=MESH)

        return carry

    lax.fori_loop(0, 2 * REACH + 1, greet, 0)
    neighbours = jnp.minimum(v, REACH) + jnp.minimum(blocks - 1 - v, REACH)

    def send(way, slot, to_slot, k, src=None):
        at = pl.ds(k * chunk, chunk)
        to = (v - 1, v + 1, v - LINE, v + LINE)[way]
        return pltpu.make_async_remote_copy(
            src_ref=raw.at[slot, at] if src is None else src.at[at], dst_ref=raw.at[to_slot, at],
            send_sem=raw_ss.at[way, slot, k], recv_sem=raw_rs.at[to_slot, k],
            device_id=(to, s), device_id_type=MESH)

    def receive(slot, k):
        send(DOWN, slot, slot, k).wait_recv()

    def own_sends(k, act):
        @pl.when(low)
        def _():
            act(send(UP, z, z, k, dosages))

        @pl.when(~low)
        def _():
            act(send(DOWN, z, z, k, dosages))

        @pl.when(~first_line & ((z == 0) | ((z >= mid) & (z < LINE - 1))))
        def _():
            act(send(BACK, z, ONE_ON, k, dosages))

        @pl.when(~last_line & (z > 0))
        def _():
            act(send(FORE, z, BEHIND, k, dosages))

    def from_above(i):
        return jnp.maximum(z + 1, mid) + i

    def from_below(i):
        return jnp.minimum(z, mid) - 1 - i

    def relay(i, k, act, wait):
        above, below = from_above(i), from_below(i)

        @pl.when((i < mid) & (above < LINE))
        def _():
            if wait:
                receive(above, k)

            @pl.when(z > 0)
            def _():
                act(send(DOWN, above, above, k))

            @pl.when(~first_line & (z >= mid) & (i == 0))
            def _():
                act(send(BACK, above, TWO_ON, k))

        @pl.when((i < mid) & (below >= 0))
        def _():
            if wait:
                receive(below, k)

            @pl.when(z < LINE - 1)
            def _():
                act(send(UP, below, below, k))

            @pl.when(~first_line & low & (below == 0))
            def _():
                act(send(BACK, below, ONE_ON, k))

            @pl.when(~first_line & (z == mid) & (i == 0))
            def _():
                act(send(BACK, below, HIGH_ON, k))

    def start(copy):
        copy.start()

    def sent(copy):
        copy.wait_send()

    def local_statistics():
        values = dosages[...].astype(f32)
        local_mean = jnp.sum(values, axis=1, keepdims=True) / cols
        centred = values - local_mean
        local_m2 = jnp.sum(centred * centred, axis=1, keepdims=True)
        lane = lax.broadcasted_iota(jnp.int32, (rows, 128), 1)
        both = jnp.where(lane == 0, local_mean, jnp.where(lane == 1, local_m2, f32(0.0)))
        stat_out[...] = both.T[0:2, :]

    local_statistics()
    pl.semaphore_wait(barrier, neighbours + smps - 1)

    for k in range(CHUNKS):
        own_sends(k, start)

    def stat_copy(step):
        peer = lax.rem(s + step, smps)
        return pltpu.make_async_remote_copy(
            src_ref=stat_out, dst_ref=stat_in.at[step], send_sem=stat_ss.at[step],
            recv_sem=stat_rs.at[step], device_id=(v, peer), device_id_type=MESH)

    for step in range(1, smps):
        stat_copy(step).start()
    stat_in[0] = stat_out[...]

    def needed(at, d):
        spot = at + d
        inside = pick(at < mid, (d < 0) | (spot >= mid), (d > 0) | (spot < mid))
        after = pick(
            at < mid,
            spot == LINE,
            (at < LINE - 1) & ((d == LINE) | (d == LINE + 1) | ((d == LINE - 1) & (at == mid))),
        )
        return pick(spot < 0, (d == -LINE) & (at > 0), pick(spot >= LINE, after, inside))

    def fact_copy(d):
        return pltpu.make_async_remote_copy(
            src_ref=facts.at[REACH], dst_ref=facts.at[REACH - d], send_sem=fact_ss.at[REACH + d],
            recv_sem=fact_rs.at[REACH - d], device_id=(v + d, s), device_id_type=MESH)

    def each_fact(act):
        def one(n, carry):
            d = n - REACH

            @pl.when(there(d) & needed((v + d + LINE) % LINE, -d))
            def _():
                act(fact_copy(d))

            return carry

        lax.fori_loop(0, 2 * REACH + 1, one, 0)

    def column(at, k):
        line_id = lax.broadcasted_iota(jnp.int32, (128, rows), 0)
        table = facts[at]
        flat = jnp.where(line_id == 0, table[k[0] : k[0] + 1], f32(0.0))
        for j in range(1, len(k)):
            flat = jnp.where(line_id == j, table[k[j] : k[j] + 1], flat)
        return flat.T

    def standardize(block, slot, d):
        flat = column(REACH + d, (0, 1))
        scaled = (block[...].astype(f32) - flat[:, 0:1]) * flat[:, 1:2]
        ready[slot] = scaled.astype(jnp.bfloat16)

    def settle():
        for step in range(1, smps):
            stat_copy(step).wait()
        gathered = stat_in[...]
        local_means = gathered[:, 0, :]
        mean = jnp.sum(local_means, axis=0, keepdims=True) / smps
        off = local_means - mean
        m2 = jnp.sum(gathered[:, 1, :] + cols * (off * off), axis=0, keepdims=True)
        place = lax.broadcasted_iota(jnp.int32, (3, rows), 0)
        scale = lax.rsqrt(m2 / total_samples + 1e-05)
        facts[REACH] = jnp.where(place == 0, mean, jnp.where(place == 1, scale, counts[...]))
        each_fact(start)
        standardize(dosages, z, 0)

        @pl.when(last_line)
        def _():
            ready[ONE_ON] = jnp.zeros((rows, cols), jnp.bfloat16)

    def take_in(slot, d, whole):
        if whole:
            for k in range(CHUNKS):
                receive(slot, k)
        fact_copy(-d).wait_recv()
        standardize(raw.at[slot], slot, d)

    def prepare(step):
        @pl.when((step < mid) & (from_above(step) < LINE))
        def _():
            take_in(from_above(step), from_above(step) - z, False)

        @pl.when((step < mid) & (from_below(step) >= 0))
        def _():
            take_in(from_below(step), from_below(step) - z, False)

        @pl.when((step == 1) & ~first_line & (z > 0))
        def _():
            take_in(BEHIND, -LINE, True)

        @pl.when((step == 2) & ~last_line & (z >= mid) & (z < LINE - 1))
        def _():
            take_in(ONE_ON, LINE, True)
            take_in(TWO_ON, LINE + 1, True)

        @pl.when((step == 2) & ~last_line & (z == mid))
        def _():
            take_in(HIGH_ON, LINE - 1, True)

        @pl.when((step == 3) & ~last_line & low)
        def _():
            take_in(ONE_ON, LINE - z, True)

    def task(family, i):
        if family == 0:
            left = jnp.maximum(z, mid) + i
            at = pick(low, jnp.minimum(i + 1, 3), i)
            return low | (i <= LINE - 2 - z), at, z, left, left + 1, left - z, i * 0
        if family == 1:
            left = jnp.minimum(z, mid - 1) - 1 - i
            return (left >= 0) & ~first_line, i + 1, BEHIND, left, left + 1, LINE + left - z, i * 0 - LINE
        if family == 2:
            holds = pick(low, i <= z - 1, (i <= LINE - 2 - z) & ~last_line)
            return (
                holds, pick(low, i, 2 + i // 2), pick(low, z - 1 - i, z + 1 + i), pick(low, z - 1, ONE_ON),
                pick(low, z, TWO_ON), pick(low, i, LINE - 1 - i), pick(low, -1 - i, 1 + i))
        below, at = z == mid - 1, z == mid
        end = ((z == 1) & (i < 2)) | ((z == 2) & (i >= 2))
        return (
            below | (at & ~last_line) | end, pick(below, i, pick(at, 2 + i // 2, 3)),
            pick(below, mid - 1 - i, mid + i), pick(below, mid - 1, pick(at, HIGH_ON, LINE - 1)),
            pick(below, mid, ONE_ON), pick(below, i, pick(at, LINE - 1 - i, mid - 1 - i)),
            pick(below, -i, pick(at, i, mid + i - z)))

    row_ids = lax.broadcasted_iota(jnp.int32, (rows, rows), 0)
    col_ids = lax.broadcasted_iota(jnp.int32, (rows, rows), 1)

    def multiply(left, right):
        return lax.dot_general(
            ready[left], ready[right], (((1,), (1,)), ((), ())), preferred_element_type=f32
        )

    def twin_copy(n):
        return pltpu.make_async_remote_copy(
            src_ref=other.at[n], dst_ref=twin.at[n], send_sem=twin_ss.at[n], recv_sem=twin_rs.at[n],
            device_id=(v, s + 1 - 2 * core), device_id_type=MESH)

    def run(n, row, left, right):
        merged = jnp.where(col_ids > row_ids, multiply(row, left), multiply(row, right))
        turned = skew(merged)
        first, second = turned[:, :width], turned[:, width:]

        @pl.when(core == 0)
        def _():
            mine[n] = first
            other[n] = second

        @pl.when(core != 0)
        def _():
            mine[n] = second
            other[n] = first

        twin_copy(n).start()

    def share_copy(n, g):
        peer = hi * (2 * YS) + lax.rem(g, YS) * 2 + core
        return pltpu.make_async_remote_copy(
            src_ref=mine.at[n], dst_ref=shares.at[n, y], send_sem=share_ss.at[n],
            recv_sem=share_rs.at[n, y], device_id=(v, peer), device_id_type=MESH)

    def fold(n, g):
        twin_copy(n).wait_recv()
        both = mine[n] + twin[n]

        @pl.when(lax.rem(g, YS) == y)
        def _():
            shares[n, y] = both

        @pl.when(lax.rem(g, YS) != y)
        def _():
            mine[n] = both
            share_copy(n, g).start()

    def gather(n):
        for step in range(1, YS):
            source = lax.rem(y + step, YS)
            pltpu.make_async_remote_copy(
                src_ref=shares.at[n, source], dst_ref=shares.at[n, source], send_sem=share_ss.at[n],
                recv_sem=share_rs.at[n, source], device_id=(v, s), device_id_type=MESH).wait_recv()
        return jnp.sum(shares[n], axis=0)

    def give_copy(n):
        return pltpu.make_async_remote_copy(
            src_ref=part.at[n], dst_ref=across.at[n], send_sem=give_ss.at[n], recv_sem=give_rs.at[n],
            device_id=(v, (1 - hi) * (2 * YS) + y * 2 + core), device_id_type=MESH)

    def give(n):
        part[n] = gather(n)
        give_copy(n).start()

    step_rows = rows // 2
    full_at = pl.ds(pl.multiple_of((1 - core) * step_rows, step_rows), rows)
    half_at = pl.ds(pl.multiple_of(core * rows, step_rows), step_rows)
    half_rows = pl.ds(pl.multiple_of((1 - core) * step_rows, step_rows), step_rows)

    def ends(n, far):
        places = []
        for j, (d, src, dst) in enumerate(
            (
                (far, part.at[n], arrived),
                (far + group + core, part.at[n], window.at[full_at]),
                (far + group + 1 - core, part.at[n, half_rows], window.at[half_at]),
            )
        ):
            copy = pltpu.make_async_remote_copy(
                src_ref=src, dst_ref=dst, send_sem=end_ss.at[n, j], recv_sem=end_rs.at[j],
                device_id=(v + d, s), device_id_type=MESH)
            places.append((d, copy))
        return places

    def take(n, far):
        total = gather(n)
        give_copy(n).wait_recv()
        total = (total + across[n]) / total_samples
        offset = lax.broadcasted_iota(jnp.int32, (rows, width), 1) + s * width
        later = lax.broadcasted_iota(jnp.int32, (rows, width), 0) + (v + far) * rows + 1 + offset
        count = column(REACH + far, (2,))[:, 0:1]
        keep = (offset.astype(f32) < count) & (later < total_rows)
        part[n] = jnp.where(keep, total, f32(0.0))
        up_to, full_to, half_to = ends(n, far)

        @pl.when(up_to[0] == 0)
        def _():
            arrived[...] = part[n]

        @pl.when(full_to[0] == 0)
        def _():
            window[full_at, :] = part[n]

        @pl.when(half_to[0] == 0)
        def _():
            window[half_at, :] = part[n, half_rows, :]

        for d, copy in (up_to, full_to, half_to):

            @pl.when(there(d))
            def _(copy=copy):
                copy.start()

    def work(phase, step):
        def each(stage, family, when):
            def one(i, carry):
                holds, at, row, left, right, g, far = task(family, i)
                n = family * mid + i
                due = holds & (at == when)
                if stage == 0:

                    @pl.when(due)
                    def _():
                        run(n, row, left, right)

                if stage == 1:

                    @pl.when(due)
                    def _():
                        fold(n, g)

                if stage == 2:

                    @pl.when(due & (lax.rem(g, YS) == y) & (g // YS != hi))
                    def _():
                        give(n)

                if stage == 3:

                    @pl.when(due & (g == group))
                    def _():
                        take(n, far)

                return carry

            lax.fori_loop(0, mid, one, 0)

        for stage, lag in enumerate((0, FOLD, GIVE, TAKE)):
            slot = phase - lag
            each(stage, slot % PHASES, step + slot // PHASES)

    early = (z < 2) | (z >= LINE - 2)

    @pl.when(early)
    def _():
        settle()

    for k in range(CHUNKS):
        relay(0, k, start, True)

    @pl.when(~early)
    def _():
        settle()

    def stream(t, carry):
        for phase in range(PHASES):
            for k in range(phase * CHUNKS // PHASES, (phase + 1) * CHUNKS // PHASES):
                relay(t, k, start, True)
            if phase == 0:
                prepare(t - 1)
            work(phase, t - 1)
        return carry

    lax.fori_loop(1, 1 + (4 * PHASES + TAKE + PHASES - 1) // PHASES, stream, 0)

    local = [False, False, False]
    for family in range(4):
        for i in range(mid):
            holds, _, _, _, _, g, far = task(family, jnp.int32(i))
            for j, d in enumerate((far, far + group + core, far + group + 1 - core)):
                local[j] = local[j] | (holds & (g == group) & (d == 0))
    exists = ~last_line | (group <= LINE - 1 - z)
    full_from, half_from = v - group - core, v - group - 1 + core
    incoming = ends(0, 0)

    @pl.when(~local[0] & exists)
    def _():
        incoming[0][1].wait_recv()

    @pl.when(~exists)
    def _():
        arrived[...] = jnp.zeros((rows, width), f32)

    upper[...] = arrived[...]

    @pl.when(full_from < 0)
    def _():
        window[full_at, :] = jnp.zeros((rows, width), f32)

    @pl.when(half_from < 0)
    def _():
        window[half_at, :] = jnp.zeros((step_rows, width), f32)

    @pl.when((full_from >= 0) & ~local[1])
    def _():
        incoming[1][1].wait_recv()

    @pl.when((half_from >= 0) & ~local[2])
    def _():
        incoming[2][1].wait_recv()

    lower[...] = unshear(window[...], rows)

    for k in range(CHUNKS):
        own_sends(k, sent)

    def relayed(m, carry):
        relay(m // CHUNKS, m % CHUNKS, sent, False)
        return carry

    lax.fori_loop(0, mid * CHUNKS, relayed, 0)
    each_fact(sent)

    for family in range(4):

        def moved(i, carry, family=family):
            holds, _, _, _, _, g, far = task(family, i)
            n = family * mid + i
            in_plane = lax.rem(g, YS) == y

            @pl.when(holds)
            def _():
                twin_copy(n).wait_send()

            @pl.when(holds & ~in_plane)
            def _():
                share_copy(n, g).wait_send()

            @pl.when(holds & in_plane & (g // YS != hi))
            def _():
                give_copy(n).wait_send()

            for d, copy in ends(n, far):

                @pl.when(holds & (g == group) & there(d))
                def _(copy=copy):
                    copy.wait_send()

            return carry

        lax.fori_loop(0, mid, moved, 0)


def per_device(dosages, band_counts):
    rows, cols = dosages.shape
    smps, blocks = lax.axis_size("smp"), lax.axis_size("var")
    width = W // smps
    f32 = jnp.float32
    counts = jnp.repeat(band_counts.astype(f32), BLK)[None, :]
    vmem = pl.BlockSpec(memory_space=pltpu.VMEM)
    dma = pltpu.SemaphoreType.DMA
    out = jax.ShapeDtypeStruct((rows, width), f32)
    tile = pltpu.VMEM((TASKS, rows, width), f32)
    return pl.pallas_call(
        functools.partial(kernel, cols * smps, rows * blocks),
        out_shape=(out, out),
        in_specs=[vmem, vmem],
        out_specs=(vmem, vmem),
        scratch_shapes=[
            pltpu.VMEM((SLOTS, rows, cols), jnp.bfloat16),
            pltpu.VMEM((SLOTS, rows, cols), jnp.bfloat16),
            tile,
            tile,
            pltpu.VMEM((TASKS, YS, rows, width), f32),
            tile,
            tile,
            tile,
            pltpu.VMEM((rows, width), f32),
            pltpu.VMEM((rows + rows // 2, width), f32),
            pltpu.VMEM((2, rows), f32),
            pltpu.VMEM((smps, 2, rows), f32),
            pltpu.VMEM((2 * REACH + 1, 3, rows), f32),
            dma((smps,)),
            dma((smps,)),
            dma((4, SLOTS, CHUNKS)),
            dma((SLOTS, CHUNKS)),
            dma((2 * REACH + 1,)),
            dma((2 * REACH + 1,)),
            dma((TASKS,)),
            dma((TASKS,)),
            dma((TASKS,)),
            dma((TASKS, YS)),
            dma((TASKS,)),
            dma((TASKS,)),
            dma((TASKS, 3)),
            dma((3,)),
        ],
        compiler_params=pltpu.CompilerParams(
            collective_id=0, has_side_effects=True, vmem_limit_bytes=56 * 2**20
        ),
        cost_estimate=pl.CostEstimate(
            flops=2 * rows * (W + rows) * cols, bytes_accessed=rows * cols * 2, transcendentals=0
        ),
    )(dosages, counts)


def solution(mesh):
    return jax.shard_map(
        per_device,
        mesh=mesh,
        in_specs=(P("var", "smp"), P("var")),
        out_specs=(P("var", "smp"), P("var", "smp")),
        check_vma=False,
    )
```

```python
import functools

import jax
import jax.numpy as jnp
from jax import lax
from jax.experimental import pallas as pl
from jax.experimental.pallas import tpu as pltpu
from jax.sharding import PartitionSpec as P

W = 2048
BLK = 128
LINE = 8
YS = 4
CHUNKS = 8
FOLD, GIVE, TAKE = 1, 3, 6
BEHIND_BY = 2
MESH = pl.DeviceIdType.MESH


def skew(tile):
    n = tile.shape[1]
    sub = lax.broadcasted_iota(jnp.int32, (8, n), 0)
    parts = []
    for at in range(0, tile.shape[0], 8):
        part = pltpu.roll(tile[at : at + 8], (2 * n - at - 1) % n, 1)
        for step in (1, 2, 4):
            part = jnp.where((sub & step) != 0, pltpu.roll(part, n - step, 1), part)
        parts.append(part)
    return jnp.concatenate(parts, 0)


def unshear(window, rows):
    height, n = window.shape
    lag = n - 1 - lax.broadcasted_iota(jnp.int32, (height, n), 1)
    step = 1
    while step < n:
        moved = pltpu.roll(window, height - step, 0)
        window = jnp.where((lag & step) != 0, moved, window)
        step *= 2
    return window[:rows]


DOWN, UP, BACK, FORE = range(4)
ONE_ON, TWO_ON, HIGH_ON, BEHIND = 8, 9, 10, 11
SLOTS = 12
REACH = 9
PHASES = 4
TASKS = 16


def kernel(
    total_samples, total_rows,
    dosages, counts, upper, lower,
    raw, ready, mine, twin, shares, part, other, across, arrived, window, stat_out, stat_in, stat_sum, facts,
    stat_ss, stat_rs, raw_ss, raw_rs, fact_ss, fact_rs,
    twin_ss, twin_rs, share_ss, share_rs, give_ss, give_rs, end_ss, end_rs,
):
    rows, cols = dosages.shape
    v = lax.axis_index("var")
    s = lax.axis_index("smp")
    x, z = v // LINE, v % LINE
    hi, y, core = s // (2 * YS), (s // 2) % YS, s % 2
    lines = total_rows // rows // LINE
    blocks = lines * LINE
    mid = LINE // 2
    group = hi * YS + y
    plane = y * 2 + core
    chunk = rows // CHUNKS
    width = upper.shape[1]
    f32 = jnp.float32
    low = z < mid
    first_line, last_line = x == 0, x == lines - 1
    pick = jnp.where

    def there(d):
        return (d != 0) & (v + d >= 0) & (v + d < blocks)

    def plane_peer(step):
        return (v, hi * (2 * YS) + lax.rem(plane + step, 2 * YS))

    barrier = pltpu.get_barrier_semaphore()
    across_peer = (v, (1 - hi) * (2 * YS) + plane)
    pl.semaphore_signal(barrier, inc=1, device_id=across_peer, device_id_type=MESH)
    for step in range(1, 2 * YS):
        pl.semaphore_signal(barrier, inc=1, device_id=plane_peer(step), device_id_type=MESH)

    def greet(n, carry):
        d = n - REACH

        @pl.when(there(d))
        def _():
            pl.semaphore_signal(barrier, inc=1, device_id=(v + d, s), device_id_type=MESH)

        return carry

    lax.fori_loop(0, 2 * REACH + 1, greet, 0)
    neighbours = jnp.minimum(v, REACH) + jnp.minimum(blocks - 1 - v, REACH)

    def send(way, slot, to_slot, k, src=None):
        at = pl.ds(k * chunk, chunk)
        to = (v - 1, v + 1, v - LINE, v + LINE)[way]
        return pltpu.make_async_remote_copy(
            src_ref=raw.at[slot, at] if src is None else src.at[at], dst_ref=raw.at[to_slot, at],
            send_sem=raw_ss.at[way, slot, k], recv_sem=raw_rs.at[to_slot, k],
            device_id=(to, s), device_id_type=MESH)

    def receive(slot, k):
        send(DOWN, slot, slot, k).wait_recv()

    def own_sends(k, act):
        @pl.when(low)
        def _():
            act(send(UP, z, z, k, dosages))

        @pl.when(~low)
        def _():
            act(send(DOWN, z, z, k, dosages))

        @pl.when(~first_line & ((z == 0) | ((z >= mid) & (z < LINE - 1))))
        def _():
            act(send(BACK, z, ONE_ON, k, dosages))

        @pl.when(~last_line & (z > 0))
        def _():
            act(send(FORE, z, BEHIND, k, dosages))

    def from_above(i):
        return jnp.maximum(z + 1, mid) + i

    def from_below(i):
        return jnp.minimum(z, mid) - 1 - i

    def relay(i, k, act, wait):
        above, below = from_above(i), from_below(i)

        @pl.when((i < mid) & (above < LINE))
        def _():
            if wait:
                receive(above, k)

            @pl.when(z > 0)
            def _():
                act(send(DOWN, above, above, k))

            @pl.when(~first_line & (z >= mid) & (i == 0))
            def _():
                act(send(BACK, above, TWO_ON, k))

        @pl.when((i < mid) & (below >= 0))
        def _():
            if wait:
                receive(below, k)

            @pl.when(z < LINE - 1)
            def _():
                act(send(UP, below, below, k))

            @pl.when(~first_line & low & (below == 0))
            def _():
                act(send(BACK, below, ONE_ON, k))

            @pl.when(~first_line & (z == mid) & (i == 0))
            def _():
                act(send(BACK, below, HIGH_ON, k))

    def start(copy):
        copy.start()

    def sent(copy):
        copy.wait_send()

    def local_statistics():
        values = dosages[...].astype(f32)
        local_mean = jnp.sum(values, axis=1, keepdims=True) / cols
        centred = values - local_mean
        local_m2 = jnp.sum(centred * centred, axis=1, keepdims=True)
        lane = lax.broadcasted_iota(jnp.int32, (rows, 128), 1)
        both = jnp.where(lane == 0, local_mean, jnp.where(lane == 1, local_m2, f32(0.0)))
        stat_out[...] = both.T[0:2, :]

    pl.semaphore_wait(barrier, neighbours + 2 * YS)

    for k in range(CHUNKS):
        own_sends(k, start)

    local_statistics()

    def stat_copy(step):
        return pltpu.make_async_remote_copy(
            src_ref=stat_out, dst_ref=stat_in.at[step], send_sem=stat_ss.at[step],
            recv_sem=stat_rs.at[step], device_id=plane_peer(step), device_id_type=MESH)

    def far_stat():
        return pltpu.make_async_remote_copy(
            src_ref=stat_sum.at[0], dst_ref=stat_sum.at[1], send_sem=stat_ss.at[0],
            recv_sem=stat_rs.at[0], device_id=across_peer, device_id_type=MESH)

    def pooled(table, samples):
        means = table[:, 0, :]
        mean = jnp.sum(means, axis=0, keepdims=True) / table.shape[0]
        off = means - mean
        return mean, jnp.sum(table[:, 1, :] + samples * (off * off), axis=0, keepdims=True)

    place = lax.broadcasted_iota(jnp.int32, (3, rows), 0)
    for step in range(1, 2 * YS):
        stat_copy(step).start()
    stat_in[0] = stat_out[...]
    for step in range(1, 2 * YS):
        stat_copy(step).wait()
    plane_mean, plane_m2 = pooled(stat_in[...], cols)
    stat_sum[0] = jnp.where(place[:2] == 0, plane_mean, plane_m2)
    far_stat().start()

    def needed(at, d):
        spot = at + d
        inside = pick(at < mid, (d < 0) | (spot >= mid), (d > 0) | (spot < mid))
        after = pick(
            at < mid,
            spot == LINE,
            (at < LINE - 1) & ((d == LINE) | (d == LINE + 1) | ((d == LINE - 1) & (at == mid))),
        )
        return pick(spot < 0, (d == -LINE) & (at > 0), pick(spot >= LINE, after, inside))

    def fact_copy(d):
        return pltpu.make_async_remote_copy(
            src_ref=facts.at[REACH], dst_ref=facts.at[REACH - d], send_sem=fact_ss.at[REACH + d],
            recv_sem=fact_rs.at[REACH - d], device_id=(v + d, s), device_id_type=MESH)

    def each_fact(act):
        def one(n, carry):
            d = n - REACH

            @pl.when(there(d) & needed((v + d + LINE) % LINE, -d))
            def _():
                act(fact_copy(d))

            return carry

        lax.fori_loop(0, 2 * REACH + 1, one, 0)

    def column(at, k):
        line_id = lax.broadcasted_iota(jnp.int32, (128, rows), 0)
        table = facts[at]
        flat = jnp.where(line_id == 0, table[k[0] : k[0] + 1], f32(0.0))
        for j in range(1, len(k)):
            flat = jnp.where(line_id == j, table[k[j] : k[j] + 1], flat)
        return flat.T

    def standardize(block, slot, d):
        flat = column(REACH + d, (0, 1))
        scaled = (block[...].astype(f32) - flat[:, 0:1]) * flat[:, 1:2]
        ready[slot] = scaled.astype(jnp.bfloat16)

    def settle():
        far_stat().wait()
        mean, m2 = pooled(stat_sum[...], cols * 2 * YS)
        scale = lax.rsqrt(m2 / total_samples + 1e-05)
        facts[REACH] = jnp.where(place == 0, mean, jnp.where(place == 1, scale, counts[...]))
        each_fact(start)
        standardize(dosages, z, 0)

        @pl.when(last_line)
        def _():
            ready[ONE_ON] = jnp.zeros((rows, cols), jnp.bfloat16)

    def take_in(slot, d, whole):
        if whole:
            for k in range(CHUNKS):
                receive(slot, k)
        fact_copy(-d).wait_recv()
        standardize(raw.at[slot], slot, d)

    def prepare(step):
        @pl.when((step < mid) & (from_above(step) < LINE))
        def _():
            take_in(from_above(step), from_above(step) - z, False)

        @pl.when((step < mid) & (from_below(step) >= 0))
        def _():
            take_in(from_below(step), from_below(step) - z, False)

        @pl.when((step == 1) & ~first_line & (z > 0))
        def _():
            take_in(BEHIND, -LINE, True)

        @pl.when((step == 2) & ~last_line & (z >= mid) & (z < LINE - 1))
        def _():
            take_in(ONE_ON, LINE, True)
            take_in(TWO_ON, LINE + 1, True)

        @pl.when((step == 2) & ~last_line & (z == mid))
        def _():
            take_in(HIGH_ON, LINE - 1, True)

        @pl.when((step == 3) & ~last_line & low)
        def _():
            take_in(ONE_ON, LINE - z, True)

    def task(family, i):
        if family == 0:
            left = jnp.maximum(z, mid) + i
            at = pick(low, jnp.minimum(i + 1, 3), i)
            return low | (i <= LINE - 2 - z), at, z, left, left + 1, left - z, i * 0
        if family == 1:
            left = jnp.minimum(z, mid - 1) - 1 - i
            return (left >= 0) & ~first_line, i + 1, BEHIND, left, left + 1, LINE + left - z, i * 0 - LINE
        if family == 2:
            holds = pick(low, i <= z - 1, (i <= LINE - 2 - z) & ~last_line)
            return (
                holds, pick(low, i, 2 + i // 2), pick(low, z - 1 - i, z + 1 + i), pick(low, z - 1, ONE_ON),
                pick(low, z, TWO_ON), pick(low, i, LINE - 1 - i), pick(low, -1 - i, 1 + i))
        below, at = z == mid - 1, z == mid
        end = ((z == 1) & (i < 2)) | ((z == 2) & (i >= 2))
        return (
            below | (at & ~last_line) | end, pick(below, i, pick(at, 2 + i // 2, 3)),
            pick(below, mid - 1 - i, mid + i), pick(below, mid - 1, pick(at, HIGH_ON, LINE - 1)),
            pick(below, mid, ONE_ON), pick(below, i, pick(at, LINE - 1 - i, mid - 1 - i)),
            pick(below, -i, pick(at, i, mid + i - z)))

    row_ids = lax.broadcasted_iota(jnp.int32, (rows, rows), 0)
    col_ids = lax.broadcasted_iota(jnp.int32, (rows, rows), 1)

    def multiply(left, right):
        return lax.dot_general(
            ready[left], ready[right], (((1,), (1,)), ((), ())), preferred_element_type=f32
        )

    def twin_copy(n):
        return pltpu.make_async_remote_copy(
            src_ref=other.at[n], dst_ref=twin.at[n], send_sem=twin_ss.at[n], recv_sem=twin_rs.at[n],
            device_id=(v, s + 1 - 2 * core), device_id_type=MESH)

    def run(n, row, left, right):
        merged = jnp.where(col_ids > row_ids, multiply(row, left), multiply(row, right))
        turned = skew(merged)
        first, second = turned[:, :width], turned[:, width:]

        @pl.when(core == 0)
        def _():
            mine[n] = first
            other[n] = second

        @pl.when(core != 0)
        def _():
            mine[n] = second
            other[n] = first

        twin_copy(n).start()

    def share_copy(n, g):
        peer = hi * (2 * YS) + lax.rem(g, YS) * 2 + core
        return pltpu.make_async_remote_copy(
            src_ref=mine.at[n], dst_ref=shares.at[n, y], send_sem=share_ss.at[n],
            recv_sem=share_rs.at[n, y], device_id=(v, peer), device_id_type=MESH)

    def fold(n, g):
        twin_copy(n).wait_recv()
        both = mine[n] + twin[n]

        @pl.when(lax.rem(g, YS) == y)
        def _():
            shares[n, y] = both

        @pl.when(lax.rem(g, YS) != y)
        def _():
            mine[n] = both
            share_copy(n, g).start()

    def gather(n):
        for step in range(1, YS):
            source = lax.rem(y + step, YS)
            pltpu.make_async_remote_copy(
                src_ref=shares.at[n, source], dst_ref=shares.at[n, source], send_sem=share_ss.at[n],
                recv_sem=share_rs.at[n, source], device_id=(v, s), device_id_type=MESH).wait_recv()
        return jnp.sum(shares[n], axis=0)

    def give_copy(n):
        return pltpu.make_async_remote_copy(
            src_ref=part.at[n], dst_ref=across.at[n], send_sem=give_ss.at[n], recv_sem=give_rs.at[n],
            device_id=across_peer, device_id_type=MESH)

    def give(n):
        part[n] = gather(n)
        give_copy(n).start()

    step_rows = rows // 2
    full_at = pl.ds(pl.multiple_of((1 - core) * step_rows, step_rows), rows)
    half_at = pl.ds(pl.multiple_of(core * rows, step_rows), step_rows)
    half_rows = pl.ds(pl.multiple_of((1 - core) * step_rows, step_rows), step_rows)

    def ends(n, far):
        places = []
        for j, (d, src, dst) in enumerate(
            (
                (far, part.at[n], arrived),
                (far + group + core, part.at[n], window.at[full_at]),
                (far + group + 1 - core, part.at[n, half_rows], window.at[half_at]),
            )
        ):
            copy = pltpu.make_async_remote_copy(
                src_ref=src, dst_ref=dst, send_sem=end_ss.at[n, j], recv_sem=end_rs.at[j],
                device_id=(v + d, s), device_id_type=MESH)
            places.append((d, copy))
        return places

    def take(n, far):
        total = gather(n)
        give_copy(n).wait_recv()
        total = (total + across[n]) / total_samples
        offset = lax.broadcasted_iota(jnp.int32, (rows, width), 1) + s * width
        later = lax.broadcasted_iota(jnp.int32, (rows, width), 0) + (v + far) * rows + 1 + offset
        count = column(REACH + far, (2,))[:, 0:1]
        keep = (offset.astype(f32) < count) & (later < total_rows)
        part[n] = jnp.where(keep, total, f32(0.0))
        up_to, full_to, half_to = ends(n, far)

        @pl.when(up_to[0] == 0)
        def _():
            arrived[...] = part[n]

        @pl.when(full_to[0] == 0)
        def _():
            window[full_at, :] = part[n]

        @pl.when(half_to[0] == 0)
        def _():
            window[half_at, :] = part[n, half_rows, :]

        for d, copy in (up_to, full_to, half_to):

            @pl.when(there(d))
            def _(copy=copy):
                copy.start()

    def sweep(stage, family, due):
        def one(i, carry):
            holds, at, row, left, right, g, far = task(family, i)
            n = family * mid + i
            now = holds & due(at * PHASES + family)
            if stage == 1:
                now = now & (lax.rem(g, YS) == y) & (g // YS != hi)
            if stage == 2:
                now = now & (g == group)

            @pl.when(now)
            def _():
                if stage == -1:
                    run(n, row, left, right)
                if stage == 0:
                    fold(n, g)
                if stage == 1:
                    give(n)
                if stage == 2:
                    take(n, far)

            return carry

        lax.fori_loop(0, mid, one, 0)

    def work(phase, step):
        for stage, lag in enumerate((0, FOLD, GIVE, TAKE)):
            family = (phase - lag) % PHASES
            when = step * PHASES + phase - lag
            sweep(stage - 1, family, lambda slot, when=when: slot == when)

    local = [False, False, False]
    for family in range(4):
        for i in range(mid):
            holds, _, _, _, _, g, far = task(family, jnp.int32(i))
            for j, d in enumerate((far, far + group + core, far + group + 1 - core)):
                local[j] = local[j] | (holds & (g == group) & (d == 0))

    early = (z < 2) | (z >= LINE - 2)

    @pl.when(early)
    def _():
        settle()

    for k in range(CHUNKS):
        relay(0, k, start, True)

    @pl.when(~early)
    def _():
        settle()

    def stream(t, carry):
        for phase in range(PHASES):
            for k in range(phase * CHUNKS // PHASES, (phase + 1) * CHUNKS // PHASES):
                relay(t, k, start, True)
            step = t - 1 + (phase - BEHIND_BY) // PHASES
            if phase == BEHIND_BY:
                prepare(step)
            work((phase - BEHIND_BY) % PHASES, step)
        return carry

    lax.fori_loop(1, mid, stream, 0)
    done = (mid - 1) * PHASES - BEHIND_BY - 1
    prepare(mid - 1)
    for family in range(4):
        sweep(-1, family, lambda slot: slot > done)
    for stage, lag in enumerate((FOLD, GIVE, TAKE)):
        for at in range(1, mid):
            for family in range(4):
                if at * PHASES + family > done - lag:
                    sweep(stage, family, lambda slot, at=at, family=family: slot == at * PHASES + family)

    exists = ~last_line | (group <= LINE - 1 - z)
    full_from, half_from = v - group - core, v - group - 1 + core
    incoming = ends(0, 0)

    @pl.when(~local[0] & exists)
    def _():
        incoming[0][1].wait_recv()

    @pl.when(~exists)
    def _():
        arrived[...] = jnp.zeros((rows, width), f32)

    upper[...] = arrived[...]

    @pl.when(full_from < 0)
    def _():
        window[full_at, :] = jnp.zeros((rows, width), f32)

    @pl.when(half_from < 0)
    def _():
        window[half_at, :] = jnp.zeros((step_rows, width), f32)

    @pl.when((full_from >= 0) & ~local[1])
    def _():
        incoming[1][1].wait_recv()

    @pl.when((half_from >= 0) & ~local[2])
    def _():
        incoming[2][1].wait_recv()

    lower[...] = unshear(window[...], rows)

    for k in range(CHUNKS):
        own_sends(k, sent)

    def relayed(m, carry):
        relay(m // CHUNKS, m % CHUNKS, sent, False)
        return carry

    lax.fori_loop(0, mid * CHUNKS, relayed, 0)
    each_fact(sent)

    for family in range(4):

        def moved(i, carry, family=family):
            holds, _, _, _, _, g, far = task(family, i)
            n = family * mid + i
            in_plane = lax.rem(g, YS) == y

            @pl.when(holds)
            def _():
                twin_copy(n).wait_send()

            @pl.when(holds & ~in_plane)
            def _():
                share_copy(n, g).wait_send()

            @pl.when(holds & in_plane & (g // YS != hi))
            def _():
                give_copy(n).wait_send()

            for d, copy in ends(n, far):

                @pl.when(holds & (g == group) & there(d))
                def _(copy=copy):
                    copy.wait_send()

            return carry

        lax.fori_loop(0, mid, moved, 0)


def per_device(dosages, band_counts):
    rows, cols = dosages.shape
    smps, blocks = lax.axis_size("smp"), lax.axis_size("var")
    width = W // smps
    f32 = jnp.float32
    counts = jnp.repeat(band_counts.astype(f32), BLK)[None, :]
    vmem = pl.BlockSpec(memory_space=pltpu.VMEM)
    dma = pltpu.SemaphoreType.DMA
    out = jax.ShapeDtypeStruct((rows, width), f32)
    tile = pltpu.VMEM((TASKS, rows, width), f32)
    return pl.pallas_call(
        functools.partial(kernel, cols * smps, rows * blocks),
        out_shape=(out, out),
        in_specs=[vmem, vmem],
        out_specs=(vmem, vmem),
        scratch_shapes=[
            pltpu.VMEM((SLOTS, rows, cols), jnp.bfloat16),
            pltpu.VMEM((SLOTS, rows, cols), jnp.bfloat16),
            tile,
            tile,
            pltpu.VMEM((TASKS, YS, rows, width), f32),
            tile,
            tile,
            tile,
            pltpu.VMEM((rows, width), f32),
            pltpu.VMEM((rows + rows // 2, width), f32),
            pltpu.VMEM((2, rows), f32),
            pltpu.VMEM((2 * YS, 2, rows), f32),
            pltpu.VMEM((2, 2, rows), f32),
            pltpu.VMEM((2 * REACH + 1, 3, rows), f32),
            dma((2 * YS,)),
            dma((2 * YS,)),
            dma((4, SLOTS, CHUNKS)),
            dma((SLOTS, CHUNKS)),
            dma((2 * REACH + 1,)),
            dma((2 * REACH + 1,)),
            dma((TASKS,)),
            dma((TASKS,)),
            dma((TASKS,)),
            dma((TASKS, YS)),
            dma((TASKS,)),
            dma((TASKS,)),
            dma((TASKS, 3)),
            dma((3,)),
        ],
        compiler_params=pltpu.CompilerParams(
            collective_id=0, has_side_effects=True, vmem_limit_bytes=38 * 2**20
        ),
        cost_estimate=pl.CostEstimate(
            flops=2 * rows * (W + rows) * cols, bytes_accessed=rows * cols * 2, transcendentals=0
        ),
    )(dosages, counts)


def solution(mesh):
    return jax.shard_map(
        per_device,
        mesh=mesh,
        in_specs=(P("var", "smp"), P("var")),
        out_specs=(P("var", "smp"), P("var", "smp")),
        check_vma=False,
    )
```

```python
import functools

import jax
import jax.numpy as jnp
from jax import lax
from jax.experimental import pallas as pl
from jax.experimental.pallas import tpu as pltpu
from jax.sharding import PartitionSpec as P

W = 2048
BLK = 128
LINE = 8
YS = 4
CHUNKS = 8
FOLD, GIVE, TAKE = 1, 3, 6
BEHIND_BY = 2
MESH = pl.DeviceIdType.MESH


def skew(tile):
    n = tile.shape[1]
    sub = lax.broadcasted_iota(jnp.int32, (8, n), 0)
    parts = []
    for at in range(0, tile.shape[0], 8):
        part = pltpu.roll(tile[at : at + 8], (2 * n - at - 1) % n, 1)
        for step in (1, 2, 4):
            part = jnp.where((sub & step) != 0, pltpu.roll(part, n - step, 1), part)
        parts.append(part)
    return jnp.concatenate(parts, 0)


def unshear(window, rows):
    height, n = window.shape
    lag = n - 1 - lax.broadcasted_iota(jnp.int32, (height, n), 1)
    step = 1
    while step < n:
        moved = pltpu.roll(window, height - step, 0)
        window = jnp.where((lag & step) != 0, moved, window)
        step *= 2
    return window[:rows]


DOWN, UP, BACK, FORE = range(4)
ONE_ON, TWO_ON, HIGH_ON, BEHIND = 8, 9, 10, 11
SLOTS = 12
REACH = 9
PHASES = 4
TASKS = 16


def kernel(
    total_samples, total_rows,
    dosages, counts, upper, lower,
    raw, ready, mine, twin, shares, part, other, across, arrived, window, stat_out, stat_in, stat_sum, facts,
    stat_ss, stat_rs, raw_ss, raw_rs, hop_rs, fact_ss, fact_rs,
    twin_ss, twin_rs, share_ss, share_rs, give_ss, give_rs, end_ss, end_rs,
):
    rows, cols = dosages.shape
    v = lax.axis_index("var")
    s = lax.axis_index("smp")
    x, z = v // LINE, v % LINE
    hi, y, core = s // (2 * YS), (s // 2) % YS, s % 2
    lines = total_rows // rows // LINE
    blocks = lines * LINE
    mid = LINE // 2
    group = hi * YS + y
    plane = y * 2 + core
    chunk = rows // CHUNKS
    width = upper.shape[1]
    f32 = jnp.float32
    low = z < mid
    first_line, last_line = x == 0, x == lines - 1
    pick = jnp.where

    def there(d):
        return (d != 0) & (v + d >= 0) & (v + d < blocks)

    def plane_peer(step):
        return (v, hi * (2 * YS) + lax.rem(plane + step, 2 * YS))

    own = raw.at[z]
    fetch = pltpu.make_async_copy(dosages, own, stat_ss.at[2 * YS])
    fetch.start()

    barrier = pltpu.get_barrier_semaphore()
    across_peer = (v, (1 - hi) * (2 * YS) + plane)
    pl.semaphore_signal(barrier, inc=1, device_id=across_peer, device_id_type=MESH)
    for step in range(1, 2 * YS):
        pl.semaphore_signal(barrier, inc=1, device_id=plane_peer(step), device_id_type=MESH)

    def greet(n, carry):
        d = n - REACH

        @pl.when(there(d))
        def _():
            pl.semaphore_signal(barrier, inc=1, device_id=(v + d, s), device_id_type=MESH)

        return carry

    lax.fori_loop(0, 2 * REACH + 1, greet, 0)
    neighbours = jnp.minimum(v, REACH) + jnp.minimum(blocks - 1 - v, REACH)

    def send(way, slot, to_slot, k, src=None):
        at = pl.ds(0, rows) if k is None else pl.ds(k * chunk, chunk)
        to = (v - 1, v + 1, v - LINE, v + LINE)[way]
        return pltpu.make_async_remote_copy(
            src_ref=raw.at[slot, at] if src is None else src.at[at], dst_ref=raw.at[to_slot, at],
            send_sem=raw_ss.at[to_slot],
            recv_sem=raw_rs.at[to_slot, 0 if k is None else k] if way in (DOWN, UP) else hop_rs.at[to_slot - LINE],
            device_id=(to, s), device_id_type=MESH)

    def receive(slot, k):
        send(DOWN, slot, slot, k).wait_recv()

    def own_sends(k, act):
        @pl.when(low)
        def _():
            act(send(UP, z, z, k, dosages))

        @pl.when(~low)
        def _():
            act(send(DOWN, z, z, k, dosages))

        @pl.when(~first_line & ((z == 0) | ((z >= mid) & (z < LINE - 1))))
        def _():
            act(send(BACK, z, ONE_ON, k, dosages))

        @pl.when(~last_line & (z > 0))
        def _():
            act(send(FORE, z, BEHIND, k, dosages))

    def from_above(i):
        return jnp.maximum(z + 1, mid) + i

    def from_below(i):
        return jnp.minimum(z, mid) - 1 - i

    def relay(i, k, act, wait):
        above, below = from_above(i), from_below(i)

        @pl.when((i < mid) & (above < LINE))
        def _():
            if wait:
                receive(above, k)

            @pl.when(z > 0)
            def _():
                act(send(DOWN, above, above, k))

            @pl.when(~first_line & (z >= mid) & (i == 0))
            def _():
                act(send(BACK, above, TWO_ON, k))

        @pl.when((i < mid) & (below >= 0))
        def _():
            if wait:
                receive(below, k)

            @pl.when(z < LINE - 1)
            def _():
                act(send(UP, below, below, k))

            @pl.when(~first_line & low & (below == 0))
            def _():
                act(send(BACK, below, ONE_ON, k))

            @pl.when(~first_line & (z == mid) & (i == 0))
            def _():
                act(send(BACK, below, HIGH_ON, k))

    def start(copy):
        copy.start()

    def sent(copy):
        copy.wait_send()

    def local_statistics():
        fetch.wait()
        values = own[...].astype(f32)
        local_mean = jnp.sum(values, axis=1, keepdims=True) / cols
        centred = values - local_mean
        local_m2 = jnp.sum(centred * centred, axis=1, keepdims=True)
        lane = lax.broadcasted_iota(jnp.int32, (rows, 128), 1)
        both = jnp.where(lane == 0, local_mean, jnp.where(lane == 1, local_m2, f32(0.0)))
        stat_out[...] = both.T[0:2, :]

    pl.semaphore_wait(barrier, neighbours + 2 * YS)

    for k in range(CHUNKS):
        own_sends(k, start)

    local_statistics()

    def stat_copy(step):
        return pltpu.make_async_remote_copy(
            src_ref=stat_out, dst_ref=stat_in.at[step], send_sem=stat_ss.at[step],
            recv_sem=stat_rs.at[step], device_id=plane_peer(step), device_id_type=MESH)

    def far_stat():
        return pltpu.make_async_remote_copy(
            src_ref=stat_sum.at[0], dst_ref=stat_sum.at[1], send_sem=stat_ss.at[0],
            recv_sem=stat_rs.at[0], device_id=across_peer, device_id_type=MESH)

    def pooled(table, samples):
        means = table[:, 0, :]
        mean = jnp.sum(means, axis=0, keepdims=True) / table.shape[0]
        off = means - mean
        return mean, jnp.sum(table[:, 1, :] + samples * (off * off), axis=0, keepdims=True)

    place = lax.broadcasted_iota(jnp.int32, (3, rows), 0)
    for step in range(1, 2 * YS):
        stat_copy(step).start()
    stat_in[0] = stat_out[...]
    for step in range(1, 2 * YS):
        stat_copy(step).wait()
    plane_mean, plane_m2 = pooled(stat_in[...], cols)
    stat_sum[0] = jnp.where(place[:2] == 0, plane_mean, plane_m2)
    far_stat().start()

    def needed(at, d):
        spot = at + d
        inside = pick(at < mid, (d < 0) | (spot >= mid), (d > 0) | (spot < mid))
        after = pick(
            at < mid,
            spot == LINE,
            (at < LINE - 1) & ((d == LINE) | (d == LINE + 1) | ((d == LINE - 1) & (at == mid))),
        )
        return pick(spot < 0, (d == -LINE) & (at > 0), pick(spot >= LINE, after, inside))

    def fact_copy(d):
        return pltpu.make_async_remote_copy(
            src_ref=facts.at[REACH], dst_ref=facts.at[REACH - d], send_sem=fact_ss.at[REACH + d],
            recv_sem=fact_rs.at[REACH - d], device_id=(v + d, s), device_id_type=MESH)

    def each_fact(act):
        def one(n, carry):
            d = n - REACH

            @pl.when(there(d) & needed((v + d + LINE) % LINE, -d))
            def _():
                act(fact_copy(d))

            return carry

        lax.fori_loop(0, 2 * REACH + 1, one, 0)

    def column(at, k):
        line_id = lax.broadcasted_iota(jnp.int32, (128, rows), 0)
        table = facts[at]
        flat = jnp.where(line_id == 0, table[k[0] : k[0] + 1], f32(0.0))
        for j in range(1, len(k)):
            flat = jnp.where(line_id == j, table[k[j] : k[j] + 1], flat)
        return flat.T

    def standardize(block, slot, d):
        flat = column(REACH + d, (0, 1))
        scaled = (block[...].astype(f32) - flat[:, 0:1]) * flat[:, 1:2]
        ready[slot] = scaled.astype(jnp.bfloat16)

    def settle():
        far_stat().wait()
        mean, m2 = pooled(stat_sum[...], cols * 2 * YS)
        lane = lax.broadcasted_iota(jnp.int32, (3, rows), 1)
        count = jnp.zeros((3, rows), jnp.int32)
        for j in range(rows // BLK):
            count = jnp.where(lane // BLK == j, counts[j], count)
        count = count.astype(f32)
        scale = lax.rsqrt(m2 / total_samples + 1e-05)
        facts[REACH] = jnp.where(place == 0, mean, jnp.where(place == 1, scale, count))
        each_fact(start)
        standardize(own, z, 0)

        @pl.when(last_line)
        def _():
            ready[ONE_ON] = jnp.zeros((rows, cols), jnp.bfloat16)

    def take_in(slot, d, whole):
        if whole:
            send(BACK, slot, slot, None).wait_recv()
        fact_copy(-d).wait_recv()
        standardize(raw.at[slot], slot, d)

    def prepare(step):
        @pl.when((step < mid) & (from_above(step) < LINE))
        def _():
            take_in(from_above(step), from_above(step) - z, False)

        @pl.when((step < mid) & (from_below(step) >= 0))
        def _():
            take_in(from_below(step), from_below(step) - z, False)

        @pl.when((step == 1) & ~first_line & (z > 0))
        def _():
            take_in(BEHIND, -LINE, True)

        @pl.when((step == 2) & ~last_line & (z >= mid) & (z < LINE - 1))
        def _():
            take_in(ONE_ON, LINE, True)
            take_in(TWO_ON, LINE + 1, True)

        @pl.when((step == 2) & ~last_line & (z == mid))
        def _():
            take_in(HIGH_ON, LINE - 1, True)

        @pl.when((step == 3) & ~last_line & low)
        def _():
            take_in(ONE_ON, LINE - z, True)

    def task(family, i):
        if family == 0:
            left = jnp.maximum(z, mid) + i
            at = pick(low, jnp.minimum(i + 1, 3), i)
            return low | (i <= LINE - 2 - z), at, z, left, left + 1, left - z, i * 0
        if family == 1:
            left = jnp.minimum(z, mid - 1) - 1 - i
            return (left >= 0) & ~first_line, i + 1, BEHIND, left, left + 1, LINE + left - z, i * 0 - LINE
        if family == 2:
            holds = pick(low, i <= z - 1, (i <= LINE - 2 - z) & ~last_line)
            return (
                holds, pick(low, i, 2 + i // 2), pick(low, z - 1 - i, z + 1 + i), pick(low, z - 1, ONE_ON),
                pick(low, z, TWO_ON), pick(low, i, LINE - 1 - i), pick(low, -1 - i, 1 + i))
        below, at = z == mid - 1, z == mid
        end = ((z == 0) & (i == 3)) | ((z == 1) & (i == 2)) | ((z == 2) & (i < 2))
        return (
            below | (at & ~last_line) | end, pick(below, i, pick(at, 2 + i // 2, 3)),
            pick(below, mid - 1 - i, mid + i), pick(below, mid - 1, pick(at, HIGH_ON, LINE - 1)),
            pick(below, mid, ONE_ON), pick(below, i, pick(at, LINE - 1 - i, mid - 1 - i)),
            pick(below, -i, pick(at, i, mid + i - z)))

    row_ids = lax.broadcasted_iota(jnp.int32, (rows, rows), 0)
    col_ids = lax.broadcasted_iota(jnp.int32, (rows, rows), 1)

    def multiply(left, right):
        return lax.dot_general(
            ready[left], ready[right], (((1,), (1,)), ((), ())), preferred_element_type=f32
        )

    def twin_copy(n):
        return pltpu.make_async_remote_copy(
            src_ref=other.at[n], dst_ref=twin.at[n], send_sem=twin_ss.at[n], recv_sem=twin_rs.at[n],
            device_id=(v, s + 1 - 2 * core), device_id_type=MESH)

    def run(n, row, left, right):
        merged = jnp.where(col_ids > row_ids, multiply(row, left), multiply(row, right))
        turned = skew(merged)
        first, second = turned[:, :width], turned[:, width:]

        @pl.when(core == 0)
        def _():
            mine[n] = first
            other[n] = second

        @pl.when(core != 0)
        def _():
            mine[n] = second
            other[n] = first

        twin_copy(n).start()

    def kept(n, g):
        return n // mid * 2 + g // YS

    def share_copy(n, g):
        to = lax.rem(g, YS)
        return pltpu.make_async_remote_copy(
            src_ref=mine.at[n], dst_ref=shares.at[kept(n, g), (y + YS - to) % YS], send_sem=share_ss.at[n],
            recv_sem=share_rs.at[kept(n, g)], device_id=(v, hi * (2 * YS) + to * 2 + core),
            device_id_type=MESH)

    def fold(n, g):
        twin_copy(n).wait_recv()
        both = mine[n] + twin[n]

        @pl.when(lax.rem(g, YS) == y)
        def _():
            shares[kept(n, g), 0] = both

        @pl.when(lax.rem(g, YS) != y)
        def _():
            mine[n] = both
            share_copy(n, g).start()

    def gather(m):
        pltpu.make_async_remote_copy(
            src_ref=shares.at[m, 1:YS], dst_ref=shares.at[m, 1:YS], send_sem=share_ss.at[0],
            recv_sem=share_rs.at[m], device_id=across_peer, device_id_type=MESH).wait_recv()
        return jnp.sum(shares[m], axis=0)

    def give_copy(m):
        return pltpu.make_async_remote_copy(
            src_ref=part.at[m], dst_ref=across.at[m], send_sem=give_ss.at[m], recv_sem=give_rs.at[m],
            device_id=across_peer, device_id_type=MESH)

    def give(m):
        part[m] = gather(m)
        give_copy(m).start()

    step_rows = rows // 2
    full_at = pl.ds(pl.multiple_of((1 - core) * step_rows, step_rows), rows)
    half_at = pl.ds(pl.multiple_of(core * rows, step_rows), step_rows)
    half_rows = pl.ds(pl.multiple_of((1 - core) * step_rows, step_rows), step_rows)

    def ends(m, far):
        places = []
        for j, (d, src, dst) in enumerate(
            (
                (far, part.at[m], arrived),
                (far + group + core, part.at[m], window.at[full_at]),
                (far + group + 1 - core, part.at[m, half_rows], window.at[half_at]),
            )
        ):
            copy = pltpu.make_async_remote_copy(
                src_ref=src, dst_ref=dst, send_sem=end_ss.at[m // 2, j], recv_sem=end_rs.at[j],
                device_id=(v + d, s), device_id_type=MESH)
            places.append((d, copy))
        return places

    def take(m, far):
        total = gather(m)
        give_copy(m).wait_recv()
        total = (total + across[m]) / total_samples
        offset = lax.broadcasted_iota(jnp.int32, (rows, width), 1) + s * width
        later = lax.broadcasted_iota(jnp.int32, (rows, width), 0) + (v + far) * rows + 1 + offset
        count = column(REACH + far, (2,))[:, 0:1]
        keep = (offset.astype(f32) < count) & (later < total_rows)
        part[m] = jnp.where(keep, total, f32(0.0))
        up_to, full_to, half_to = ends(m, far)

        @pl.when(up_to[0] == 0)
        def _():
            arrived[...] = part[m]

        @pl.when(full_to[0] == 0)
        def _():
            window[full_at, :] = part[m]

        @pl.when(half_to[0] == 0)
        def _():
            window[half_at, :] = part[m, half_rows, :]

        for d, copy in (full_to, half_to, up_to):

            @pl.when(there(d))
            def _(copy=copy):
                copy.start()

    def span(family, at):
        if family == 0:
            low_end = pick(at >= mid - 1, mid, at)
            lo = pick(low, at - 1, at)
            hi_ = pick(low, low_end, jnp.minimum(at + 1, LINE - 1 - z))
            return lo, pick((at > 0) | ~low, hi_, lo)
        if family == 1:
            return at - 1, pick((at > 0) & (at <= jnp.minimum(z, mid - 1)) & ~first_line, at, at - 1)
        if family == 2:
            lo = pick(low, at, 2 * (at - 2))
            return lo, pick(low, jnp.minimum(at + 1, z), pick(last_line | (at < 2), lo, jnp.minimum(lo + 2, LINE - 1 - z)))
        at_mid = (z == mid) & (at >= 2) & ~last_line
        end = (z < mid - 1) & (at == mid - 1)
        lo = pick(z == mid - 1, at, pick(z == mid, 2 * (at - 2), pick(z == 2, 0, mid - 1 - z)))
        return lo, lo + pick(z == mid - 1, 1, pick(at_mid, 2, pick(end, pick(z == 2, 2, 1), 0)))

    def sweep(stage, family, step):
        def one(i, carry):
            _, _, row, left, right, g, far = task(family, i)
            n = family * mid + i
            if stage == 0:
                run(n, row, left, right)
            if stage == 1:
                fold(n, g)
            if stage == 2:

                @pl.when((lax.rem(g, YS) == y) & (g // YS != hi))
                def _():
                    give(kept(n, g))

            if stage == 3:

                @pl.when(g == group)
                def _():
                    take(kept(n, g), far)

            return carry

        lo, up_to = span(family, step)
        lax.fori_loop(lo, pick(step >= 0, up_to, lo), one, 0)

    lags = (0, FOLD, GIVE, TAKE)

    def work(phase, step):
        for stage, lag in enumerate(lags):
            sweep(stage, (phase - lag) % PHASES, step + (phase - lag) // PHASES)

    settle_at = pick((z == 0) | (z == LINE - 1), 0, pick((z == 1) | (z == LINE - 2), CHUNKS // 2, CHUNKS))

    def opening(k, carry):
        @pl.when(k == settle_at)
        def _():
            settle()

        @pl.when(k < CHUNKS)
        def _():
            relay(0, k, start, True)

        return carry

    lax.fori_loop(0, CHUNKS + 1, opening, 0)

    def stream(t, carry):
        for phase in range(PHASES):
            for k in range(phase * CHUNKS // PHASES, (phase + 1) * CHUNKS // PHASES):
                relay(t, k, start, True)
            step = t - 1 + (phase - BEHIND_BY) // PHASES
            if phase == BEHIND_BY:
                prepare(step)
            work((phase - BEHIND_BY) % PHASES, step)
        return carry

    lax.fori_loop(1, mid, stream, 0)
    done = (mid - 1) * PHASES - BEHIND_BY
    tail = [(2, 2), (2, 3), (3, 3), (3, 0), (3, 1), (3, 2)]
    prepare(mid - 1)
    for at, family in tail:
        sweep(0, family, at)
    for stage, lag in enumerate(lags):
        if stage:
            for slot in range(done - lag, done):
                sweep(stage, slot % PHASES, slot // PHASES)
            for at, family in tail:
                sweep(stage, family, at)

    own_sends(None, sent)

    def relayed(i, carry):
        relay(i, None, sent, False)
        return carry

    lax.fori_loop(0, mid, relayed, 0)
    each_fact(sent)

    def moved(family, act):
        def one(i, carry):
            holds, _, _, _, _, g, far = task(family, i)

            @pl.when(holds)
            def _():
                act(family * mid + i, g, far)

            return carry

        lax.fori_loop(0, mid, one, 0)

    def reduced(n, g, far):
        twin_copy(n).wait_send()

        @pl.when(lax.rem(g, YS) != y)
        def _():
            share_copy(n, g).wait_send()

        @pl.when((lax.rem(g, YS) == y) & (g // YS != hi))
        def _():
            give_copy(kept(n, g)).wait_send()

    def ended(n, g, far):
        @pl.when(g == group)
        def _():
            for d, copy in ends(kept(n, g), far):

                @pl.when(there(d))
                def _(copy=copy):
                    copy.wait_send()

    for family in range(4):
        moved(family, reduced)

    exists = ~last_line | (group <= LINE - 1 - z)

    def tile_here(before):
        one_before = low & (z > 0) & ((group < z) | ((group == LINE - 1) & ~first_line))
        at_once = ((z == mid - 1) & (group < mid)) | (~low & (z < LINE - 1) & (group == 0))
        return pick(before == 1, one_before, at_once)

    local = [
        pick(low, (group >= mid - z) & (group < LINE - z), group < LINE - 1 - z)
        | ((z == mid - 1) & (group == 0))
        | ((z == mid) & (group == LINE - 1) & ~last_line),
        tile_here(core),
        tile_here(1 - core),
    ]
    full_from, half_from = v - group - core, v - group - 1 + core
    incoming = ends(0, 0)

    @pl.when(~local[0] & exists)
    def _():
        incoming[0][1].wait_recv()

    @pl.when(~exists)
    def _():
        arrived[...] = jnp.zeros((rows, width), f32)

    upper[...] = arrived[...]

    @pl.when(full_from < 0)
    def _():
        window[full_at, :] = jnp.zeros((rows, width), f32)

    @pl.when(half_from < 0)
    def _():
        window[half_at, :] = jnp.zeros((step_rows, width), f32)

    @pl.when((full_from >= 0) & ~local[1])
    def _():
        incoming[1][1].wait_recv()

    @pl.when((half_from >= 0) & ~local[2])
    def _():
        incoming[2][1].wait_recv()

    lower[...] = unshear(window[...], rows)

    for family in range(4):
        moved(family, ended)


def per_device(dosages, band_counts):
    rows, cols = dosages.shape
    smps, blocks = lax.axis_size("smp"), lax.axis_size("var")
    width = W // smps
    f32 = jnp.float32
    vmem = pl.BlockSpec(memory_space=pltpu.VMEM)
    dma = pltpu.SemaphoreType.DMA
    out = jax.ShapeDtypeStruct((rows, width), f32)
    tiles = pltpu.VMEM((TASKS, rows, width), f32)
    sums = pltpu.VMEM((8, rows, width), f32)
    return pl.pallas_call(
        functools.partial(kernel, cols * smps, rows * blocks),
        out_shape=(out, out),
        in_specs=[pl.BlockSpec(memory_space=pl.ANY), pl.BlockSpec(memory_space=pltpu.SMEM)],
        out_specs=(vmem, vmem),
        scratch_shapes=[
            pltpu.VMEM((SLOTS, rows, cols), jnp.bfloat16),
            pltpu.VMEM((SLOTS, rows, cols), jnp.bfloat16),
            tiles,
            tiles,
            pltpu.VMEM((8, YS, rows, width), f32),
            sums,
            tiles,
            sums,
            pltpu.VMEM((rows, width), f32),
            pltpu.VMEM((rows + rows // 2, width), f32),
            pltpu.VMEM((2, rows), f32),
            pltpu.VMEM((2 * YS, 2, rows), f32),
            pltpu.VMEM((2, 2, rows), f32),
            pltpu.VMEM((2 * REACH + 1, 3, rows), f32),
            dma((2 * YS + 1,)),
            dma((2 * YS,)),
            dma((SLOTS,)),
            dma((LINE, CHUNKS)),
            dma((SLOTS - LINE,)),
            dma((2 * REACH + 1,)),
            dma((2 * REACH + 1,)),
            dma((TASKS,)),
            dma((TASKS,)),
            dma((TASKS,)),
            dma((8,)),
            dma((8,)),
            dma((8,)),
            dma((4, 3)),
            dma((3,)),
        ],
        compiler_params=pltpu.CompilerParams(
            collective_id=0, has_side_effects=True, vmem_limit_bytes=32 * 2**20
        ),
        cost_estimate=pl.CostEstimate(
            flops=2 * rows * (W + rows) * cols, bytes_accessed=rows * cols * 2, transcendentals=0
        ),
    )(dosages, band_counts)


def solution(mesh):
    return jax.shard_map(
        per_device,
        mesh=mesh,
        in_specs=(P("var", "smp"), P("var")),
        out_specs=(P("var", "smp"), P("var", "smp")),
        check_vma=False,
    )
```

```python
import functools

import jax
import jax.numpy as jnp
from jax import lax
from jax.experimental import pallas as pl
from jax.experimental.pallas import tpu as pltpu
from jax.sharding import PartitionSpec as P

W = 2048
BLK = 128
LINE = 8
YS = 4
CHUNKS = 8
FOLD, GIVE, TAKE = 1, 3, 9
BEHIND_BY = 2
MESH = pl.DeviceIdType.MESH


def skew(tile):
    n = tile.shape[1]
    sub = lax.broadcasted_iota(jnp.int32, (8, n), 0)
    parts = []
    for at in range(0, tile.shape[0], 8):
        part = pltpu.roll(tile[at : at + 8], (2 * n - at - 1) % n, 1)
        for step in (1, 2, 4):
            part = jnp.where((sub & step) != 0, pltpu.roll(part, n - step, 1), part)
        parts.append(part)
    return jnp.concatenate(parts, 0)


def unshear(window, rows):
    height, n = window.shape
    lag = n - 1 - lax.broadcasted_iota(jnp.int32, (height, n), 1)
    step = 1
    while step < n:
        moved = pltpu.roll(window, height - step, 0)
        window = jnp.where((lag & step) != 0, moved, window)
        step *= 2
    return window[:rows]


DOWN, UP, BACK, FORE = range(4)
ONE_ON, TWO_ON, HIGH_ON, BEHIND = 8, 9, 10, 11
SLOTS = 12
REACH = 9
PHASES = 4
TASKS = 16


def kernel(
    total_samples, total_rows,
    dosages, counts, upper, lower,
    raw, ready, mine, twin, shares, part, other, across, arrived, window, stat_out, stat_in, stat_sum, facts,
    stat_ss, stat_rs, raw_ss, raw_rs, hop_rs, fact_ss, fact_rs,
    twin_ss, twin_rs, share_ss, share_rs, give_ss, give_rs, end_ss, end_rs,
):
    rows, cols = dosages.shape
    v = lax.axis_index("var")
    s = lax.axis_index("smp")
    x, z = v // LINE, v % LINE
    hi, y, core = s // (2 * YS), (s // 2) % YS, s % 2
    lines = total_rows // rows // LINE
    blocks = lines * LINE
    mid = LINE // 2
    group = hi * YS + y
    plane = y * 2 + core
    chunk = rows // CHUNKS
    width = upper.shape[1]
    f32 = jnp.float32
    low = z < mid
    first_line, last_line = x == 0, x == lines - 1
    pick = jnp.where

    def there(d):
        return (d != 0) & (v + d >= 0) & (v + d < blocks)

    def plane_peer(step):
        return (v, hi * (2 * YS) + lax.rem(plane + step, 2 * YS))

    own = raw.at[z]
    fetch = pltpu.make_async_copy(dosages, own, stat_ss.at[2 * YS])
    fetch.start()

    barrier = pltpu.get_barrier_semaphore()
    across_peer = (v, (1 - hi) * (2 * YS) + plane)
    pl.semaphore_signal(barrier, inc=1, device_id=across_peer, device_id_type=MESH)
    for step in range(1, 2 * YS):
        pl.semaphore_signal(barrier, inc=1, device_id=plane_peer(step), device_id_type=MESH)

    def greet(n, carry):
        d = n - REACH

        @pl.when(there(d))
        def _():
            pl.semaphore_signal(barrier, inc=1, device_id=(v + d, s), device_id_type=MESH)

        return carry

    lax.fori_loop(0, 2 * REACH + 1, greet, 0)
    neighbours = jnp.minimum(v, REACH) + jnp.minimum(blocks - 1 - v, REACH)

    def send(way, slot, to_slot, k, src=None):
        at = pl.ds(0, rows) if k is None else pl.ds(k * chunk, chunk)
        to = (v - 1, v + 1, v - LINE, v + LINE)[way]
        return pltpu.make_async_remote_copy(
            src_ref=raw.at[slot, at] if src is None else src.at[at], dst_ref=raw.at[to_slot, at],
            send_sem=raw_ss.at[to_slot],
            recv_sem=raw_rs.at[to_slot, 0 if k is None else k] if way in (DOWN, UP) else hop_rs.at[to_slot - LINE],
            device_id=(to, s), device_id_type=MESH)

    def receive(slot, k):
        send(DOWN, slot, slot, k).wait_recv()

    def own_sends(k, act):
        @pl.when(low)
        def _():
            act(send(UP, z, z, k, dosages))

        @pl.when(~low)
        def _():
            act(send(DOWN, z, z, k, dosages))

        @pl.when(~first_line & ((z == 0) | ((z >= mid) & (z < LINE - 1))))
        def _():
            act(send(BACK, z, ONE_ON, k, dosages))

        @pl.when(~last_line & (z > 0))
        def _():
            act(send(FORE, z, BEHIND, k, dosages))

    def from_above(i):
        return jnp.maximum(z + 1, mid) + i

    def from_below(i):
        return jnp.minimum(z, mid) - 1 - i

    def relay(i, k, act, wait):
        above, below = from_above(i), from_below(i)

        @pl.when((i < mid) & (above < LINE))
        def _():
            if wait:
                receive(above, k)

            @pl.when(z > 0)
            def _():
                act(send(DOWN, above, above, k))

            @pl.when(~first_line & (z >= mid) & (i == 0))
            def _():
                act(send(BACK, above, TWO_ON, k))

        @pl.when((i < mid) & (below >= 0))
        def _():
            if wait:
                receive(below, k)

            @pl.when(z < LINE - 1)
            def _():
                act(send(UP, below, below, k))

            @pl.when(~first_line & low & (below == 0))
            def _():
                act(send(BACK, below, ONE_ON, k))

            @pl.when(~first_line & (z == mid) & (i == 0))
            def _():
                act(send(BACK, below, HIGH_ON, k))

    def start(copy):
        copy.start()

    def sent(copy):
        copy.wait_send()

    def local_statistics():
        fetch.wait()
        values = own[...].astype(f32)
        local_mean = jnp.sum(values, axis=1, keepdims=True) / cols
        centred = values - local_mean
        local_m2 = jnp.sum(centred * centred, axis=1, keepdims=True)
        lane = lax.broadcasted_iota(jnp.int32, (rows, 128), 1)
        both = jnp.where(lane == 0, local_mean, jnp.where(lane == 1, local_m2, f32(0.0)))
        stat_out[...] = both.T[0:2, :]

    pl.semaphore_wait(barrier, neighbours + 2 * YS)

    for k in range(CHUNKS):
        own_sends(k, start)

    local_statistics()

    def stat_copy(step):
        return pltpu.make_async_remote_copy(
            src_ref=stat_out, dst_ref=stat_in.at[step], send_sem=stat_ss.at[step],
            recv_sem=stat_rs.at[step], device_id=plane_peer(step), device_id_type=MESH)

    def far_stat():
        return pltpu.make_async_remote_copy(
            src_ref=stat_sum.at[0], dst_ref=stat_sum.at[1], send_sem=stat_ss.at[0],
            recv_sem=stat_rs.at[0], device_id=across_peer, device_id_type=MESH)

    def pooled(table, samples):
        means = table[:, 0, :]
        mean = jnp.sum(means, axis=0, keepdims=True) / table.shape[0]
        off = means - mean
        return mean, jnp.sum(table[:, 1, :] + samples * (off * off), axis=0, keepdims=True)

    place = lax.broadcasted_iota(jnp.int32, (3, rows), 0)
    for step in range(1, 2 * YS):
        stat_copy(step).start()
    stat_in[0] = stat_out[...]
    for step in range(1, 2 * YS):
        stat_copy(step).wait()
    plane_mean, plane_m2 = pooled(stat_in[...], cols)
    stat_sum[0] = jnp.where(place[:2] == 0, plane_mean, plane_m2)
    far_stat().start()

    def needed(at, d):
        spot = at + d
        inside = pick(at < mid, (d < 0) | (spot >= mid), (d > 0) | (spot < mid))
        after = pick(
            at < mid,
            spot == LINE,
            (at < LINE - 1) & ((d == LINE) | (d == LINE + 1) | ((d == LINE - 1) & (at == mid))),
        )
        return pick(spot < 0, (d == -LINE) & (at > 0), pick(spot >= LINE, after, inside))

    def fact_copy(d):
        return pltpu.make_async_remote_copy(
            src_ref=facts.at[REACH], dst_ref=facts.at[REACH - d], send_sem=fact_ss.at[REACH + d],
            recv_sem=fact_rs.at[REACH - d], device_id=(v + d, s), device_id_type=MESH)

    def each_fact(act):
        def one(n, carry):
            d = n - REACH

            @pl.when(there(d) & needed((v + d + LINE) % LINE, -d))
            def _():
                act(fact_copy(d))

            return carry

        lax.fori_loop(0, 2 * REACH + 1, one, 0)

    def column(at, k):
        line_id = lax.broadcasted_iota(jnp.int32, (128, rows), 0)
        table = facts[at]
        flat = jnp.where(line_id == 0, table[k[0] : k[0] + 1], f32(0.0))
        for j in range(1, len(k)):
            flat = jnp.where(line_id == j, table[k[j] : k[j] + 1], flat)
        return flat.T

    def standardize(block, slot, d):
        flat = column(REACH + d, (0, 1))
        scaled = (block[...].astype(f32) - flat[:, 0:1]) * flat[:, 1:2]
        ready[slot] = scaled.astype(jnp.bfloat16)

    def settle():
        far_stat().wait()
        mean, m2 = pooled(stat_sum[...], cols * 2 * YS)
        lane = lax.broadcasted_iota(jnp.int32, (3, rows), 1)
        count = jnp.zeros((3, rows), jnp.int32)
        for j in range(rows // BLK):
            count = jnp.where(lane // BLK == j, counts[j], count)
        count = count.astype(f32)
        scale = lax.rsqrt(m2 / total_samples + 1e-05)
        facts[REACH] = jnp.where(place == 0, mean, jnp.where(place == 1, scale, count))
        each_fact(start)
        standardize(own, z, 0)

        @pl.when(last_line)
        def _():
            ready[ONE_ON] = jnp.zeros((rows, cols), jnp.bfloat16)

    def take_in(slot, d, whole):
        if whole:
            send(BACK, slot, slot, None).wait_recv()
        fact_copy(-d).wait_recv()
        standardize(raw.at[slot], slot, d)

    def prepare(step):
        @pl.when((step < mid) & (from_above(step) < LINE))
        def _():
            take_in(from_above(step), from_above(step) - z, False)

        @pl.when((step < mid) & (from_below(step) >= 0))
        def _():
            take_in(from_below(step), from_below(step) - z, False)

        @pl.when((step == 1) & ~first_line & (z > 0))
        def _():
            take_in(BEHIND, -LINE, True)

        @pl.when((step == 2) & ~last_line & (z >= mid) & (z < LINE - 1))
        def _():
            take_in(ONE_ON, LINE, True)
            take_in(TWO_ON, LINE + 1, True)

        @pl.when((step == 2) & ~last_line & (z == mid))
        def _():
            take_in(HIGH_ON, LINE - 1, True)

        @pl.when((step == 3) & ~last_line & low)
        def _():
            take_in(ONE_ON, LINE - z, True)

    def task(family, i):
        if family == 0:
            left = jnp.maximum(z, mid) + i
            at = pick(low, jnp.minimum(i + 1, 3), i)
            return low | (i <= LINE - 2 - z), at, z, left, left + 1, left - z, i * 0
        if family == 1:
            left = jnp.minimum(z, mid - 1) - 1 - i
            return (left >= 0) & ~first_line, i + 1, BEHIND, left, left + 1, LINE + left - z, i * 0 - LINE
        if family == 2:
            holds = pick(low, i <= z - 1, (i <= LINE - 2 - z) & ~last_line)
            return (
                holds, pick(low, i, 2 + i // 2), pick(low, z - 1 - i, z + 1 + i), pick(low, z - 1, ONE_ON),
                pick(low, z, TWO_ON), pick(low, i, LINE - 1 - i), pick(low, -1 - i, 1 + i))
        below, at = z == mid - 1, z == mid
        end = ((z == 0) & (i == 3)) | ((z == 1) & (i == 2)) | ((z == 2) & (i < 2))
        return (
            below | (at & ~last_line) | end, pick(below, i, pick(at, 2 + i // 2, 3)),
            pick(below, mid - 1 - i, mid + i), pick(below, mid - 1, pick(at, HIGH_ON, LINE - 1)),
            pick(below, mid, ONE_ON), pick(below, i, pick(at, LINE - 1 - i, mid - 1 - i)),
            pick(below, -i, pick(at, i, mid + i - z)))

    row_ids = lax.broadcasted_iota(jnp.int32, (rows, rows), 0)
    col_ids = lax.broadcasted_iota(jnp.int32, (rows, rows), 1)

    def multiply(left, right):
        return lax.dot_general(
            ready[left], ready[right], (((1,), (1,)), ((), ())), preferred_element_type=f32
        )

    def twin_copy(n):
        return pltpu.make_async_remote_copy(
            src_ref=other.at[n], dst_ref=twin.at[n], send_sem=twin_ss.at[n], recv_sem=twin_rs.at[n],
            device_id=(v, s + 1 - 2 * core), device_id_type=MESH)

    def run(n, row, left, right):
        merged = jnp.where(col_ids > row_ids, multiply(row, left), multiply(row, right))
        turned = skew(merged)
        first, second = turned[:, :width], turned[:, width:]

        @pl.when(core == 0)
        def _():
            mine[n] = first
            other[n] = second

        @pl.when(core != 0)
        def _():
            mine[n] = second
            other[n] = first

        twin_copy(n).start()

    def kept(n, g):
        return n // mid * 2 + g // YS

    def share_copy(n, g):
        to = lax.rem(g, YS)
        return pltpu.make_async_remote_copy(
            src_ref=mine.at[n], dst_ref=shares.at[kept(n, g), (y + YS - to) % YS], send_sem=share_ss.at[n],
            recv_sem=share_rs.at[kept(n, g)], device_id=(v, hi * (2 * YS) + to * 2 + core),
            device_id_type=MESH)

    def fold(n, g):
        twin_copy(n).wait_recv()
        both = mine[n] + twin[n]

        @pl.when(lax.rem(g, YS) == y)
        def _():
            shares[kept(n, g), 0] = both

        @pl.when(lax.rem(g, YS) != y)
        def _():
            mine[n] = both
            share_copy(n, g).start()

    def gather(m):
        pltpu.make_async_remote_copy(
            src_ref=shares.at[m, 1:YS], dst_ref=shares.at[m, 1:YS], send_sem=share_ss.at[0],
            recv_sem=share_rs.at[m], device_id=across_peer, device_id_type=MESH).wait_recv()
        return jnp.sum(shares[m], axis=0)

    def give_copy(m):
        return pltpu.make_async_remote_copy(
            src_ref=part.at[m], dst_ref=across.at[m], send_sem=give_ss.at[m], recv_sem=give_rs.at[m],
            device_id=across_peer, device_id_type=MESH)

    def give(m):
        part[m] = gather(m)
        give_copy(m).start()

    step_rows = rows // 2
    full_at = pl.ds(pl.multiple_of((1 - core) * step_rows, step_rows), rows)
    half_at = pl.ds(pl.multiple_of(core * rows, step_rows), step_rows)
    half_rows = pl.ds(pl.multiple_of((1 - core) * step_rows, step_rows), step_rows)

    def ends(m, far):
        places = []
        for j, (d, src, dst) in enumerate(
            (
                (far, part.at[m], arrived),
                (far + group + core, part.at[m], window.at[full_at]),
                (far + group + 1 - core, part.at[m, half_rows], window.at[half_at]),
            )
        ):
            copy = pltpu.make_async_remote_copy(
                src_ref=src, dst_ref=dst, send_sem=end_ss.at[m // 2, j], recv_sem=end_rs.at[j],
                device_id=(v + d, s), device_id_type=MESH)
            places.append((d, copy))
        return places

    def take(m, far):
        total = gather(m)
        give_copy(m).wait_recv()
        total = (total + across[m]) / total_samples
        offset = lax.broadcasted_iota(jnp.int32, (rows, width), 1) + s * width
        later = lax.broadcasted_iota(jnp.int32, (rows, width), 0) + (v + far) * rows + 1 + offset
        count = column(REACH + far, (2,))[:, 0:1]
        keep = (offset.astype(f32) < count) & (later < total_rows)
        part[m] = jnp.where(keep, total, f32(0.0))
        up_to, full_to, half_to = ends(m, far)

        @pl.when(up_to[0] == 0)
        def _():
            arrived[...] = part[m]

        @pl.when(full_to[0] == 0)
        def _():
            window[full_at, :] = part[m]

        @pl.when(half_to[0] == 0)
        def _():
            window[half_at, :] = part[m, half_rows, :]

        for d, copy in (full_to, half_to, up_to):

            @pl.when(there(d))
            def _(copy=copy):
                copy.start()

    def span(family, at):
        if family == 0:
            low_end = pick(at >= mid - 1, mid, at)
            lo = pick(low, at - 1, at)
            hi_ = pick(low, low_end, jnp.minimum(at + 1, LINE - 1 - z))
            return lo, pick((at > 0) | ~low, hi_, lo)
        if family == 1:
            return at - 1, pick((at > 0) & (at <= jnp.minimum(z, mid - 1)) & ~first_line, at, at - 1)
        if family == 2:
            lo = pick(low, at, 2 * (at - 2))
            return lo, pick(low, jnp.minimum(at + 1, z), pick(last_line | (at < 2), lo, jnp.minimum(lo + 2, LINE - 1 - z)))
        at_mid = (z == mid) & (at >= 2) & ~last_line
        end = (z < mid - 1) & (at == mid - 1)
        lo = pick(z == mid - 1, at, pick(z == mid, 2 * (at - 2), pick(z == 2, 0, mid - 1 - z)))
        return lo, lo + pick(z == mid - 1, 1, pick(at_mid, 2, pick(end, pick(z == 2, 2, 1), 0)))

    def sweep(stage, family, step):
        def one(i, carry):
            _, _, row, left, right, g, far = task(family, i)
            n = family * mid + i
            if stage == 0:
                run(n, row, left, right)
            if stage == 1:
                fold(n, g)
            if stage == 2:

                @pl.when((lax.rem(g, YS) == y) & (g // YS != hi))
                def _():
                    give(kept(n, g))

            if stage == 3:

                @pl.when(g == group)
                def _():
                    take(kept(n, g), far)

            return carry

        lo, up_to = span(family, step)
        lax.fori_loop(lo, pick(step >= 0, up_to, lo), one, 0)

    lags = (0, FOLD, GIVE, TAKE)

    def work(phase, step):
        for stage, lag in enumerate(lags):
            sweep(stage, (phase - lag) % PHASES, step + (phase - lag) // PHASES)

    settle_at = pick((z == 0) | (z == LINE - 1), 0, pick((z == 1) | (z == LINE - 2), CHUNKS // 2, CHUNKS))

    def opening(k, carry):
        @pl.when(k == settle_at)
        def _():
            settle()

        @pl.when(k < CHUNKS)
        def _():
            relay(0, k, start, True)

        return carry

    lax.fori_loop(0, CHUNKS + 1, opening, 0)

    def stream(t, carry):
        for phase in range(PHASES):
            for k in range(phase * CHUNKS // PHASES, (phase + 1) * CHUNKS // PHASES):
                relay(t, k, start, True)
            step = t - 1 + (phase - BEHIND_BY) // PHASES
            if phase == BEHIND_BY:
                prepare(step)
            work((phase - BEHIND_BY) % PHASES, step)
        return carry

    lax.fori_loop(1, mid, stream, 0)
    done = (mid - 1) * PHASES - BEHIND_BY
    tail = [(3, 1), (3, 0), (2, 2), (2, 3), (3, 3), (3, 2)]
    prepare(mid - 1)
    for at, family in tail:
        sweep(0, family, at)
    for stage, lag in enumerate(lags):
        if stage:
            for slot in range(done - lag, done):
                sweep(stage, slot % PHASES, slot // PHASES)
            for at, family in tail:
                sweep(stage, family, at)

    own_sends(None, sent)

    def relayed(i, carry):
        relay(i, None, sent, False)
        return carry

    lax.fori_loop(0, mid, relayed, 0)
    each_fact(sent)

    def moved(family, act):
        def one(i, carry):
            holds, _, _, _, _, g, far = task(family, i)

            @pl.when(holds)
            def _():
                act(family * mid + i, g, far)

            return carry

        lax.fori_loop(0, mid, one, 0)

    def reduced(n, g, far):
        twin_copy(n).wait_send()

        @pl.when(lax.rem(g, YS) != y)
        def _():
            share_copy(n, g).wait_send()

        @pl.when((lax.rem(g, YS) == y) & (g // YS != hi))
        def _():
            give_copy(kept(n, g)).wait_send()

    def ended(n, g, far):
        @pl.when(g == group)
        def _():
            for d, copy in ends(kept(n, g), far):

                @pl.when(there(d))
                def _(copy=copy):
                    copy.wait_send()

    for family in range(4):
        moved(family, reduced)

    exists = ~last_line | (group <= LINE - 1 - z)

    def tile_here(before):
        one_before = low & (z > 0) & ((group < z) | ((group == LINE - 1) & ~first_line))
        at_once = ((z == mid - 1) & (group < mid)) | (~low & (z < LINE - 1) & (group == 0))
        return pick(before == 1, one_before, at_once)

    local = [
        pick(low, (group >= mid - z) & (group < LINE - z), group < LINE - 1 - z)
        | ((z == mid - 1) & (group == 0))
        | ((z == mid) & (group == LINE - 1) & ~last_line),
        tile_here(core),
        tile_here(1 - core),
    ]
    full_from, half_from = v - group - core, v - group - 1 + core
    incoming = ends(0, 0)

    @pl.when(~local[0] & exists)
    def _():
        incoming[0][1].wait_recv()

    @pl.when(~exists)
    def _():
        arrived[...] = jnp.zeros((rows, width), f32)

    upper[...] = arrived[...]

    @pl.when(full_from < 0)
    def _():
        window[full_at, :] = jnp.zeros((rows, width), f32)

    @pl.when(half_from < 0)
    def _():
        window[half_at, :] = jnp.zeros((step_rows, width), f32)

    @pl.when((full_from >= 0) & ~local[1])
    def _():
        incoming[1][1].wait_recv()

    @pl.when((half_from >= 0) & ~local[2])
    def _():
        incoming[2][1].wait_recv()

    lower[...] = unshear(window[...], rows)

    for family in range(4):
        moved(family, ended)


def per_device(dosages, band_counts):
    rows, cols = dosages.shape
    smps, blocks = lax.axis_size("smp"), lax.axis_size("var")
    width = W // smps
    f32 = jnp.float32
    vmem = pl.BlockSpec(memory_space=pltpu.VMEM)
    dma = pltpu.SemaphoreType.DMA
    out = jax.ShapeDtypeStruct((rows, width), f32)
    tiles = pltpu.VMEM((TASKS, rows, width), f32)
    sums = pltpu.VMEM((8, rows, width), f32)
    return pl.pallas_call(
        functools.partial(kernel, cols * smps, rows * blocks),
        out_shape=(out, out),
        in_specs=[pl.BlockSpec(memory_space=pl.ANY), pl.BlockSpec(memory_space=pltpu.SMEM)],
        out_specs=(vmem, vmem),
        scratch_shapes=[
            pltpu.VMEM((SLOTS, rows, cols), jnp.bfloat16),
            pltpu.VMEM((SLOTS, rows, cols), jnp.bfloat16),
            tiles,
            tiles,
            pltpu.VMEM((8, YS, rows, width), f32),
            sums,
            tiles,
            sums,
            pltpu.VMEM((rows, width), f32),
            pltpu.VMEM((rows + rows // 2, width), f32),
            pltpu.VMEM((2, rows), f32),
            pltpu.VMEM((2 * YS, 2, rows), f32),
            pltpu.VMEM((2, 2, rows), f32),
            pltpu.VMEM((2 * REACH + 1, 3, rows), f32),
            dma((2 * YS + 1,)),
            dma((2 * YS,)),
            dma((SLOTS,)),
            dma((LINE, CHUNKS)),
            dma((SLOTS - LINE,)),
            dma((2 * REACH + 1,)),
            dma((2 * REACH + 1,)),
            dma((TASKS,)),
            dma((TASKS,)),
            dma((TASKS,)),
            dma((8,)),
            dma((8,)),
            dma((8,)),
            dma((4, 3)),
            dma((3,)),
        ],
        compiler_params=pltpu.CompilerParams(
            collective_id=0, has_side_effects=True, vmem_limit_bytes=32 * 2**20
        ),
        cost_estimate=pl.CostEstimate(
            flops=2 * rows * (W + rows) * cols, bytes_accessed=rows * cols * 2, transcendentals=0
        ),
    )(dosages, band_counts)


def solution(mesh):
    return jax.shard_map(
        per_device,
        mesh=mesh,
        in_specs=(P("var", "smp"), P("var")),
        out_specs=(P("var", "smp"), P("var", "smp")),
        check_vma=False,
    )
```

```python
import functools

import jax
import jax.numpy as jnp
from jax import lax
from jax.experimental import pallas as pl
from jax.experimental.pallas import tpu as pltpu
from jax.sharding import PartitionSpec as P

W = 2048
BLK = 128
LINE = 8
YS = 4
CHUNKS = 8
FOLD, GIVE, TAKE = 1, 3, 9
BEHIND_BY = 2
MESH = pl.DeviceIdType.MESH


def skew(tile):
    n = tile.shape[1]
    sub = lax.broadcasted_iota(jnp.int32, (8, n), 0)
    parts = []
    for at in range(0, tile.shape[0], 8):
        part = pltpu.roll(tile[at : at + 8], (2 * n - at - 1) % n, 1)
        for step in (1, 2, 4):
            part = jnp.where((sub & step) != 0, pltpu.roll(part, n - step, 1), part)
        parts.append(part)
    return jnp.concatenate(parts, 0)


def unshear(window, rows):
    height, n = window.shape
    lag = n - 1 - lax.broadcasted_iota(jnp.int32, (height, n), 1)
    step = 1
    while step < n:
        moved = pltpu.roll(window, height - step, 0)
        window = jnp.where((lag & step) != 0, moved, window)
        step *= 2
    return window[:rows]


DOWN, UP, BACK, FORE = range(4)
ONE_ON, TWO_ON, HIGH_ON, BEHIND = 8, 9, 10, 11
SLOTS = 12
REACH = 9
PHASES = 4
TASKS = 16


def kernel(
    total_samples, total_rows,
    dosages, counts, upper, lower,
    raw, ready, mine, twin, shares, part, other, across, arrived, window, stat_out, stat_in, stat_sum, facts,
    stat_ss, stat_rs, raw_ss, raw_rs, hop_rs, fact_ss, fact_rs,
    twin_ss, twin_rs, share_ss, share_rs, give_ss, give_rs, end_ss, end_rs,
):
    rows, cols = dosages.shape
    v = lax.axis_index("var")
    s = lax.axis_index("smp")
    x, z = v // LINE, v % LINE
    hi, y, core = s // (2 * YS), (s // 2) % YS, s % 2
    lines = total_rows // rows // LINE
    blocks = lines * LINE
    mid = LINE // 2
    group = hi * YS + y
    plane = y * 2 + core
    chunk = rows // CHUNKS
    width = upper.shape[1]
    f32 = jnp.float32
    low = z < mid
    first_line, last_line = x == 0, x == lines - 1
    pick = jnp.where

    def there(d):
        return (d != 0) & (v + d >= 0) & (v + d < blocks)

    def plane_peer(step):
        return (v, hi * (2 * YS) + lax.rem(plane + step, 2 * YS))

    own = raw.at[z]
    fetch = pltpu.make_async_copy(dosages, own, stat_ss.at[2 * YS])
    fetch.start()

    barrier = pltpu.get_barrier_semaphore()
    across_peer = (v, (1 - hi) * (2 * YS) + plane)
    pl.semaphore_signal(barrier, inc=1, device_id=across_peer, device_id_type=MESH)
    for step in range(1, 2 * YS):
        pl.semaphore_signal(barrier, inc=1, device_id=plane_peer(step), device_id_type=MESH)

    def greet(n, carry):
        d = n - REACH

        @pl.when(there(d))
        def _():
            pl.semaphore_signal(barrier, inc=1, device_id=(v + d, s), device_id_type=MESH)

        return carry

    lax.fori_loop(0, 2 * REACH + 1, greet, 0)
    neighbours = jnp.minimum(v, REACH) + jnp.minimum(blocks - 1 - v, REACH)

    def send(way, slot, to_slot, k, src=None):
        at = pl.ds(0, rows) if k is None else pl.ds(k * chunk, chunk)
        to = (v - 1, v + 1, v - LINE, v + LINE)[way]
        return pltpu.make_async_remote_copy(
            src_ref=raw.at[slot, at] if src is None else src.at[at], dst_ref=raw.at[to_slot, at],
            send_sem=raw_ss.at[to_slot],
            recv_sem=raw_rs.at[to_slot, 0 if k is None else k] if way in (DOWN, UP) else hop_rs.at[to_slot - LINE],
            device_id=(to, s), device_id_type=MESH)

    def receive(slot, k):
        send(DOWN, slot, slot, k).wait_recv()

    def own_sends(k, act):
        @pl.when(low)
        def _():
            act(send(UP, z, z, k, dosages))

        @pl.when(~low)
        def _():
            act(send(DOWN, z, z, k, dosages))

        @pl.when(~first_line & ((z == 0) | ((z >= mid) & (z < LINE - 1))))
        def _():
            act(send(BACK, z, ONE_ON, k, dosages))

        @pl.when(~last_line & (z > 0))
        def _():
            act(send(FORE, z, BEHIND, k, dosages))

    def from_above(i):
        return jnp.maximum(z + 1, mid) + i

    def from_below(i):
        return jnp.minimum(z, mid) - 1 - i

    def relay(i, k, act, wait):
        above, below = from_above(i), from_below(i)

        @pl.when((i < mid) & (above < LINE))
        def _():
            if wait:
                receive(above, k)

            @pl.when(z > 0)
            def _():
                act(send(DOWN, above, above, k))

            @pl.when(~first_line & (z >= mid) & (i == 0))
            def _():
                act(send(BACK, above, TWO_ON, k))

        @pl.when((i < mid) & (below >= 0))
        def _():
            if wait:
                receive(below, k)

            @pl.when(z < LINE - 1)
            def _():
                act(send(UP, below, below, k))

            @pl.when(~first_line & low & (below == 0))
            def _():
                act(send(BACK, below, ONE_ON, k))

            @pl.when(~first_line & (z == mid) & (i == 0))
            def _():
                act(send(BACK, below, HIGH_ON, k))

    def start(copy):
        copy.start()

    def sent(copy):
        copy.wait_send()

    def local_statistics():
        fetch.wait()
        values = own[...].astype(f32)
        local_mean = jnp.sum(values, axis=1, keepdims=True) / cols
        centred = values - local_mean
        local_m2 = jnp.sum(centred * centred, axis=1, keepdims=True)
        lane = lax.broadcasted_iota(jnp.int32, (rows, 128), 1)
        both = jnp.where(lane == 0, local_mean, jnp.where(lane == 1, local_m2, f32(0.0)))
        stat_out[...] = both.T[0:2, :]

    @pl.when(hi == 0)
    def _():
        local_statistics()

    pl.semaphore_wait(barrier, neighbours + 2 * YS)

    for k in range(CHUNKS):
        own_sends(k, start)

    @pl.when(hi != 0)
    def _():
        local_statistics()

    def stat_copy(step):
        return pltpu.make_async_remote_copy(
            src_ref=stat_out, dst_ref=stat_in.at[step], send_sem=stat_ss.at[step],
            recv_sem=stat_rs.at[step], device_id=plane_peer(step), device_id_type=MESH)

    def far_stat():
        return pltpu.make_async_remote_copy(
            src_ref=stat_sum.at[0], dst_ref=stat_sum.at[1], send_sem=stat_ss.at[0],
            recv_sem=stat_rs.at[0], device_id=across_peer, device_id_type=MESH)

    def pooled(table, samples):
        means = table[:, 0, :]
        mean = jnp.sum(means, axis=0, keepdims=True) / table.shape[0]
        off = means - mean
        return mean, jnp.sum(table[:, 1, :] + samples * (off * off), axis=0, keepdims=True)

    place = lax.broadcasted_iota(jnp.int32, (3, rows), 0)
    for step in range(1, 2 * YS):
        stat_copy(step).start()
    stat_in[0] = stat_out[...]
    for step in range(1, 2 * YS):
        stat_copy(step).wait()
    plane_mean, plane_m2 = pooled(stat_in[...], cols)
    stat_sum[0] = jnp.where(place[:2] == 0, plane_mean, plane_m2)
    far_stat().start()

    def needed(at, d):
        spot = at + d
        inside = pick(at < mid, (d < 0) | (spot >= mid), (d > 0) | (spot < mid))
        after = pick(
            at < mid,
            spot == LINE,
            (at < LINE - 1) & ((d == LINE) | (d == LINE + 1) | ((d == LINE - 1) & (at == mid))),
        )
        return pick(spot < 0, (d == -LINE) & (at > 0), pick(spot >= LINE, after, inside))

    def fact_copy(d):
        return pltpu.make_async_remote_copy(
            src_ref=facts.at[REACH], dst_ref=facts.at[REACH - d], send_sem=fact_ss.at[REACH + d],
            recv_sem=fact_rs.at[REACH - d], device_id=(v + d, s), device_id_type=MESH)

    def each_fact(act):
        def one(n, carry):
            d = n - REACH

            @pl.when(there(d) & needed((v + d + LINE) % LINE, -d))
            def _():
                act(fact_copy(d))

            return carry

        lax.fori_loop(0, 2 * REACH + 1, one, 0)

    def column(at, k):
        line_id = lax.broadcasted_iota(jnp.int32, (128, rows), 0)
        table = facts[at]
        flat = jnp.where(line_id == 0, table[k[0] : k[0] + 1], f32(0.0))
        for j in range(1, len(k)):
            flat = jnp.where(line_id == j, table[k[j] : k[j] + 1], flat)
        return flat.T

    def standardize(block, slot, d):
        flat = column(REACH + d, (0, 1))
        scaled = (block[...].astype(f32) - flat[:, 0:1]) * flat[:, 1:2]
        ready[slot] = scaled.astype(jnp.bfloat16)

    def settle():
        far_stat().wait()
        mean, m2 = pooled(stat_sum[...], cols * 2 * YS)
        lane = lax.broadcasted_iota(jnp.int32, (3, rows), 1)
        count = jnp.zeros((3, rows), jnp.int32)
        for j in range(rows // BLK):
            count = jnp.where(lane // BLK == j, counts[j], count)
        count = count.astype(f32)
        scale = lax.rsqrt(m2 / total_samples + 1e-05)
        facts[REACH] = jnp.where(place == 0, mean, jnp.where(place == 1, scale, count))
        each_fact(start)
        standardize(own, z, 0)

        @pl.when(last_line)
        def _():
            ready[ONE_ON] = jnp.zeros((rows, cols), jnp.bfloat16)

    def take_in(slot, d, whole):
        if whole:
            send(BACK, slot, slot, None).wait_recv()
        fact_copy(-d).wait_recv()
        standardize(raw.at[slot], slot, d)

    def prepare(step):
        @pl.when((step < mid) & (from_above(step) < LINE))
        def _():
            take_in(from_above(step), from_above(step) - z, False)

        @pl.when((step < mid) & (from_below(step) >= 0))
        def _():
            take_in(from_below(step), from_below(step) - z, False)

        @pl.when((step == 1) & ~first_line & (z > 0))
        def _():
            take_in(BEHIND, -LINE, True)

        @pl.when((step == 2) & ~last_line & (z >= mid) & (z < LINE - 1))
        def _():
            take_in(ONE_ON, LINE, True)
            take_in(TWO_ON, LINE + 1, True)

        @pl.when((step == 2) & ~last_line & (z == mid))
        def _():
            take_in(HIGH_ON, LINE - 1, True)

        @pl.when((step == 3) & ~last_line & low)
        def _():
            take_in(ONE_ON, LINE - z, True)

    def task(family, i):
        if family == 0:
            left = jnp.maximum(z, mid) + i
            at = pick(low, jnp.minimum(i + 1, 3), i)
            return low | (i <= LINE - 2 - z), at, z, left, left + 1, left - z, i * 0
        if family == 1:
            left = jnp.minimum(z, mid - 1) - 1 - i
            return (left >= 0) & ~first_line, i + 1, BEHIND, left, left + 1, LINE + left - z, i * 0 - LINE
        if family == 2:
            holds = pick(low, i <= z - 1, (i <= LINE - 2 - z) & ~last_line)
            return (
                holds, pick(low, i, 2 + i // 2), pick(low, z - 1 - i, z + 1 + i), pick(low, z - 1, ONE_ON),
                pick(low, z, TWO_ON), pick(low, i, LINE - 1 - i), pick(low, -1 - i, 1 + i))
        below, at = z == mid - 1, z == mid
        end = ((z == 0) & (i == 3)) | ((z == 1) & (i == 2)) | ((z == 2) & (i < 2))
        return (
            below | (at & ~last_line) | end, pick(below, i, pick(at, 2 + i // 2, 3)),
            pick(below, mid - 1 - i, mid + i), pick(below, mid - 1, pick(at, HIGH_ON, LINE - 1)),
            pick(below, mid, ONE_ON), pick(below, i, pick(at, LINE - 1 - i, mid - 1 - i)),
            pick(below, -i, pick(at, i, mid + i - z)))

    row_ids = lax.broadcasted_iota(jnp.int32, (rows, rows), 0)
    col_ids = lax.broadcasted_iota(jnp.int32, (rows, rows), 1)

    def multiply(left, right):
        return lax.dot_general(
            ready[left], ready[right], (((1,), (1,)), ((), ())), preferred_element_type=f32
        )

    def twin_copy(n):
        return pltpu.make_async_remote_copy(
            src_ref=other.at[n], dst_ref=twin.at[n], send_sem=twin_ss.at[n], recv_sem=twin_rs.at[n],
            device_id=(v, s + 1 - 2 * core), device_id_type=MESH)

    def run(n, row, left, right):
        merged = jnp.where(col_ids > row_ids, multiply(row, left), multiply(row, right))
        turned = skew(merged)
        first, second = turned[:, :width], turned[:, width:]

        @pl.when(core == 0)
        def _():
            mine[n] = first
            other[n] = second

        @pl.when(core != 0)
        def _():
            mine[n] = second
            other[n] = first

        twin_copy(n).start()

    def kept(n, g):
        return n // mid * 2 + g // YS

    def share_copy(n, g):
        to = lax.rem(g, YS)
        return pltpu.make_async_remote_copy(
            src_ref=mine.at[n], dst_ref=shares.at[kept(n, g), (y + YS - to) % YS], send_sem=share_ss.at[n],
            recv_sem=share_rs.at[kept(n, g)], device_id=(v, hi * (2 * YS) + to * 2 + core),
            device_id_type=MESH)

    def fold(n, g):
        twin_copy(n).wait_recv()
        both = mine[n] + twin[n]

        @pl.when(lax.rem(g, YS) == y)
        def _():
            shares[kept(n, g), 0] = both

        @pl.when(lax.rem(g, YS) != y)
        def _():
            mine[n] = both
            share_copy(n, g).start()

    def gather(m):
        pltpu.make_async_remote_copy(
            src_ref=shares.at[m, 1:YS], dst_ref=shares.at[m, 1:YS], send_sem=share_ss.at[0],
            recv_sem=share_rs.at[m], device_id=across_peer, device_id_type=MESH).wait_recv()
        return jnp.sum(shares[m], axis=0)

    def give_copy(m):
        return pltpu.make_async_remote_copy(
            src_ref=part.at[m], dst_ref=across.at[m], send_sem=give_ss.at[m], recv_sem=give_rs.at[m],
            device_id=across_peer, device_id_type=MESH)

    def give(m):
        part[m] = gather(m)
        give_copy(m).start()

    step_rows = rows // 2
    full_at = pl.ds(pl.multiple_of((1 - core) * step_rows, step_rows), rows)
    half_at = pl.ds(pl.multiple_of(core * rows, step_rows), step_rows)
    half_rows = pl.ds(pl.multiple_of((1 - core) * step_rows, step_rows), step_rows)

    def ends(m, far):
        places = []
        for j, (d, src, dst) in enumerate(
            (
                (far, part.at[m], arrived),
                (far + group + core, part.at[m], window.at[full_at]),
                (far + group + 1 - core, part.at[m, half_rows], window.at[half_at]),
            )
        ):
            copy = pltpu.make_async_remote_copy(
                src_ref=src, dst_ref=dst, send_sem=end_ss.at[m // 2, j], recv_sem=end_rs.at[j],
                device_id=(v + d, s), device_id_type=MESH)
            places.append((d, copy))
        return places

    def take(m, far):
        total = gather(m)
        give_copy(m).wait_recv()
        total = (total + across[m]) / total_samples
        offset = lax.broadcasted_iota(jnp.int32, (rows, width), 1) + s * width
        later = lax.broadcasted_iota(jnp.int32, (rows, width), 0) + (v + far) * rows + 1 + offset
        count = column(REACH + far, (2,))[:, 0:1]
        keep = (offset.astype(f32) < count) & (later < total_rows)
        part[m] = jnp.where(keep, total, f32(0.0))
        up_to, full_to, half_to = ends(m, far)

        @pl.when(up_to[0] == 0)
        def _():
            arrived[...] = part[m]

        @pl.when(full_to[0] == 0)
        def _():
            window[full_at, :] = part[m]

        @pl.when(half_to[0] == 0)
        def _():
            window[half_at, :] = part[m, half_rows, :]

        for d, copy in (full_to, half_to, up_to):

            @pl.when(there(d))
            def _(copy=copy):
                copy.start()

    def span(family, at):
        if family == 0:
            low_end = pick(at >= mid - 1, mid, at)
            lo = pick(low, at - 1, at)
            hi_ = pick(low, low_end, jnp.minimum(at + 1, LINE - 1 - z))
            return lo, pick((at > 0) | ~low, hi_, lo)
        if family == 1:
            return at - 1, pick((at > 0) & (at <= jnp.minimum(z, mid - 1)) & ~first_line, at, at - 1)
        if family == 2:
            lo = pick(low, at, 2 * (at - 2))
            return lo, pick(low, jnp.minimum(at + 1, z), pick(last_line | (at < 2), lo, jnp.minimum(lo + 2, LINE - 1 - z)))
        at_mid = (z == mid) & (at >= 2) & ~last_line
        end = (z < mid - 1) & (at == mid - 1)
        lo = pick(z == mid - 1, at, pick(z == mid, 2 * (at - 2), pick(z == 2, 0, mid - 1 - z)))
        return lo, lo + pick(z == mid - 1, 1, pick(at_mid, 2, pick(end, pick(z == 2, 2, 1), 0)))

    def sweep(stage, family, step):
        def one(i, carry):
            _, _, row, left, right, g, far = task(family, i)
            n = family * mid + i
            if stage == 0:
                run(n, row, left, right)
            if stage == 1:
                fold(n, g)
            if stage == 2:

                @pl.when((lax.rem(g, YS) == y) & (g // YS != hi))
                def _():
                    give(kept(n, g))

            if stage == 3:

                @pl.when(g == group)
                def _():
                    take(kept(n, g), far)

            return carry

        lo, up_to = span(family, step)
        lax.fori_loop(lo, pick(step >= 0, up_to, lo), one, 0)

    lags = (0, FOLD, GIVE, TAKE)

    def work(phase, step):
        for stage, lag in enumerate(lags):
            sweep(stage, (phase - lag) % PHASES, step + (phase - lag) // PHASES)

    settle_at = pick((z == 0) | (z == LINE - 1), 0, pick((z == 1) | (z == LINE - 2), CHUNKS // 2, CHUNKS))

    def opening(k, carry):
        @pl.when(k == settle_at)
        def _():
            settle()

        @pl.when(k < CHUNKS)
        def _():
            relay(0, k, start, True)

        return carry

    lax.fori_loop(0, CHUNKS + 1, opening, 0)

    def stream(t, carry):
        for phase in range(PHASES):
            for k in range(phase * CHUNKS // PHASES, (phase + 1) * CHUNKS // PHASES):
                relay(t, k, start, True)
            step = t - 1 + (phase - BEHIND_BY) // PHASES
            if phase == BEHIND_BY:
                prepare(step)
            work((phase - BEHIND_BY) % PHASES, step)
        return carry

    lax.fori_loop(1, mid, stream, 0)
    done = (mid - 1) * PHASES - BEHIND_BY
    tail = [(3, 1), (2, 2), (2, 3), (3, 3), (3, 0), (3, 2)]
    prepare(mid - 1)
    for at, family in tail:
        sweep(0, family, at)
    for stage, lag in enumerate(lags):
        if stage:
            for slot in range(done - lag, done):
                sweep(stage, slot % PHASES, slot // PHASES)
            for at, family in tail:
                sweep(stage, family, at)

    own_sends(None, sent)

    def relayed(i, carry):
        relay(i, None, sent, False)
        return carry

    lax.fori_loop(0, mid, relayed, 0)
    each_fact(sent)

    def moved(family, act):
        def one(i, carry):
            holds, _, _, _, _, g, far = task(family, i)

            @pl.when(holds)
            def _():
                act(family * mid + i, g, far)

            return carry

        lax.fori_loop(0, mid, one, 0)

    def reduced(n, g, far):
        twin_copy(n).wait_send()

        @pl.when(lax.rem(g, YS) != y)
        def _():
            share_copy(n, g).wait_send()

        @pl.when((lax.rem(g, YS) == y) & (g // YS != hi))
        def _():
            give_copy(kept(n, g)).wait_send()

    def ended(n, g, far):
        @pl.when(g == group)
        def _():
            for d, copy in ends(kept(n, g), far):

                @pl.when(there(d))
                def _(copy=copy):
                    copy.wait_send()

    for family in range(4):
        moved(family, reduced)

    exists = ~last_line | (group <= LINE - 1 - z)

    def tile_here(before):
        one_before = low & (z > 0) & ((group < z) | ((group == LINE - 1) & ~first_line))
        at_once = ((z == mid - 1) & (group < mid)) | (~low & (z < LINE - 1) & (group == 0))
        return pick(before == 1, one_before, at_once)

    local = [
        pick(low, (group >= mid - z) & (group < LINE - z), group < LINE - 1 - z)
        | ((z == mid - 1) & (group == 0))
        | ((z == mid) & (group == LINE - 1) & ~last_line),
        tile_here(core),
        tile_here(1 - core),
    ]
    full_from, half_from = v - group - core, v - group - 1 + core
    incoming = ends(0, 0)

    @pl.when(~local[0] & exists)
    def _():
        incoming[0][1].wait_recv()

    @pl.when(~exists)
    def _():
        arrived[...] = jnp.zeros((rows, width), f32)

    upper[...] = arrived[...]

    @pl.when(full_from < 0)
    def _():
        window[full_at, :] = jnp.zeros((rows, width), f32)

    @pl.when(half_from < 0)
    def _():
        window[half_at, :] = jnp.zeros((step_rows, width), f32)

    @pl.when((full_from >= 0) & ~local[1])
    def _():
        incoming[1][1].wait_recv()

    @pl.when((half_from >= 0) & ~local[2])
    def _():
        incoming[2][1].wait_recv()

    lower[...] = unshear(window[...], rows)

    for family in range(4):
        moved(family, ended)


def per_device(dosages, band_counts):
    rows, cols = dosages.shape
    smps, blocks = lax.axis_size("smp"), lax.axis_size("var")
    width = W // smps
    f32 = jnp.float32
    vmem = pl.BlockSpec(memory_space=pltpu.VMEM)
    dma = pltpu.SemaphoreType.DMA
    out = jax.ShapeDtypeStruct((rows, width), f32)
    tiles = pltpu.VMEM((TASKS, rows, width), f32)
    sums = pltpu.VMEM((8, rows, width), f32)
    return pl.pallas_call(
        functools.partial(kernel, cols * smps, rows * blocks),
        out_shape=(out, out),
        in_specs=[pl.BlockSpec(memory_space=pl.ANY), pl.BlockSpec(memory_space=pltpu.SMEM)],
        out_specs=(vmem, vmem),
        scratch_shapes=[
            pltpu.VMEM((SLOTS, rows, cols), jnp.bfloat16),
            pltpu.VMEM((SLOTS, rows, cols), jnp.bfloat16),
            tiles,
            tiles,
            pltpu.VMEM((8, YS, rows, width), f32),
            sums,
            tiles,
            sums,
            pltpu.VMEM((rows, width), f32),
            pltpu.VMEM((rows + rows // 2, width), f32),
            pltpu.VMEM((2, rows), f32),
            pltpu.VMEM((2 * YS, 2, rows), f32),
            pltpu.VMEM((2, 2, rows), f32),
            pltpu.VMEM((2 * REACH + 1, 3, rows), f32),
            dma((2 * YS + 1,)),
            dma((2 * YS,)),
            dma((SLOTS,)),
            dma((LINE, CHUNKS)),
            dma((SLOTS - LINE,)),
            dma((2 * REACH + 1,)),
            dma((2 * REACH + 1,)),
            dma((TASKS,)),
            dma((TASKS,)),
            dma((TASKS,)),
            dma((8,)),
            dma((8,)),
            dma((8,)),
            dma((4, 3)),
            dma((3,)),
        ],
        compiler_params=pltpu.CompilerParams(
            collective_id=0, has_side_effects=True, vmem_limit_bytes=32 * 2**20
        ),
        cost_estimate=pl.CostEstimate(
            flops=2 * rows * (W + rows) * cols, bytes_accessed=rows * cols * 2, transcendentals=0
        ),
    )(dosages, band_counts)


def solution(mesh):
    return jax.shard_map(
        per_device,
        mesh=mesh,
        in_specs=(P("var", "smp"), P("var")),
        out_specs=(P("var", "smp"), P("var", "smp")),
        check_vma=False,
    )
```
